512 devices in a mesh: section: 16 (over x, y), expert: 32 (over z, core).
Axes of the slice: x: 4, y: 4, z: 16, core: 2. Of those that a mesh axis runs over, the one named last changes fastest.
Arguments:
- stream: bfloat16 [16, 4096, 2560], P('section', 'expert'), may hold values from -6 to 6
- lengths: int32 [16, 16], P('section'), may hold values from 64 to 256, as said below
- routes: int32 [2, 16, 4096, 2], P(None, 'section', 'expert'), may hold values from 0 to 63, as said below
- norm_gains: bfloat16 [16, 2560], P('section'), may hold values from 0.099609375 to 1.8984375
- router_weights: bfloat16 [16, 2560, 64], P('section'), may hold values from -0.125 to 0.125
- up_weights: bfloat16 [16, 2560, 10240], P('section', None, 'expert'), may hold values from -0.125 to 0.125
- down_weights: bfloat16 [16, 10240, 2560], P('section', 'expert'), may hold values from -0.0625 to 0.0625
Outputs:
- advanced: bfloat16 [16, 4096, 2560], P('section', 'expert')
The draws below stay inside these ranges and needn't reach their ends.
Inputs may be any that keep to these rules, and one draw needn't show every extreme that they name: Each row names two different experts. In each aligned block of 128 rows of routes[t, s] (the rows of one device), exactly 12 rows name expert s. An input is 256 consecutive token rows of a micro-batch; its first lengths tokens are live.
All inputs are finite; a program needn't handle non-finite values.
Results may differ from the reference program's by a relative error of at most 0.0045.
Values may be sent and summed in bfloat16 or wider, within the bound.
A program may use at most 64 MiB of HBM per device.

```python
import jax
import jax.numpy as jnp
from jax import lax

D = 2560
HID = 10240
EXPERTS = 64
SEQ = 256
TOK_DEV = 128
SECTIONS = 16
TOKENS = 4096
INPUTS = 16
CAP = 12


def draw_lengths(key, part):
    key = jax.random.fold_in(key, 11)
    key_values, key_order = jax.random.split(key)
    count_all = SECTIONS * INPUTS
    values = jax.random.randint(key_values, (count_all,), SEQ // 4, SEQ + 1)
    order = jax.random.permutation(key_order, count_all)
    values = jnp.where(order == 0, SEQ, values)
    values = jnp.where(order == 1, SEQ // 4, values)
    return values.reshape(SECTIONS, INPUTS).astype(jnp.int32)


def draw_routes(key, part):
    key = jax.random.fold_in(key, 23)
    key_score, key_first, key_second, key_column = jax.random.split(key, 4)
    shape = (2, SECTIONS, TOKENS // TOK_DEV, TOK_DEV)
    scores = jax.random.randint(key_score, shape, 0, 1 << 20) * TOK_DEV + jnp.arange(TOK_DEV, dtype=jnp.int32)
    ranks = jnp.argsort(jnp.argsort(scores, axis=-1), axis=-1)
    marked = ranks < CAP
    first = jax.random.randint(key_first, shape, 0, EXPERTS - 1)
    second = jax.random.randint(key_second, shape, 0, EXPERTS - 2)
    second = second + (second >= first).astype(jnp.int32)
    window = jnp.arange(SECTIONS, dtype=jnp.int32)[None, :, None, None]
    first = first + (first >= window).astype(jnp.int32)
    second = second + (second >= window).astype(jnp.int32)
    column = jax.random.randint(key_column, shape, 0, 2)
    left = jnp.where(marked, jnp.where(column == 0, window, first), first)
    right = jnp.where(marked, jnp.where(column == 0, first, window), second)
    paired = jnp.stack([left, right], axis=-1)
    return paired.reshape(2, SECTIONS, TOKENS, 2).astype(jnp.int32)


def block_levels(stream_key, dims, cuts, low, largest):
    level, own = 1.0, jax.random.fold_in(stream_key, 6)
    for dim, blocks in cuts:
        heights = jnp.exp(jax.random.uniform(jax.random.fold_in(own, dim), (blocks,), jnp.float32, low / len(cuts), largest / len(cuts)))
        level = level * jnp.repeat(heights, dims[dim] // blocks).reshape([-1 if axis == dim else 1 for axis in range(len(dims))])
    return level


def scatter_about(own_key, shape, deviation, limit, pieces=(), held_as=jnp.bfloat16):
    drawn = deviation * jax.random.normal(own_key, shape, jnp.float32)
    if pieces:
        drawn = drawn * block_levels(own_key, shape, pieces, -0.22, 0.18)
    return jnp.clip(drawn, -limit, limit).astype(held_as)


def setup_inputs(seed: int = 0) -> dict:
    arg_keys = jax.random.split(jax.random.key(seed), 8)
    stream = scatter_about(arg_keys[0], (SECTIONS, TOKENS, D), 1.0, 6.0, ((0, 16), (1, 32)))
    lengths = draw_lengths(jax.random.fold_in(arg_keys[7], 71), 0)
    routes = draw_routes(jax.random.fold_in(arg_keys[7], 71), 0)
    norm_gains = jnp.clip(1.0 + 0.18 * jax.random.normal(arg_keys[3], (SECTIONS, D), jnp.float32), 0.099609375, 1.8984375).astype(jnp.bfloat16)
    router_weights = scatter_about(arg_keys[4], (SECTIONS, D, EXPERTS), D ** -0.5, 0.125, ((0, 16),))
    up_weights = scatter_about(arg_keys[5], (SECTIONS, D, HID), D ** -0.5, 0.125, ((0, 16), (2, 32)))
    down_weights = scatter_about(arg_keys[6], (SECTIONS, HID, D), HID ** -0.5, 0.0625, ((0, 16), (1, 32)))
    return {"stream": stream, "lengths": lengths, "routes": routes, "norm_gains": norm_gains, "router_weights": router_weights, "up_weights": up_weights, "down_weights": down_weights}


EPSILON = 1e-06

def normalize(hidden, gain_row):
    widened = hidden.astype(jnp.float32)
    mean_square = lax.optimization_barrier(jnp.mean(widened * widened, axis=-1, keepdims=True))
    scaled = widened * lax.rsqrt(mean_square + EPSILON) * gain_row.astype(jnp.float32)[None, :]
    return (widened, scaled.astype(jnp.bfloat16))

def gate_pair(normed, router_matrix, chosen):
    logits = jnp.dot(normed, router_matrix, preferred_element_type=jnp.float32)
    expert_total = router_matrix.shape[1]
    picked = (chosen[:, :, None] == jnp.arange(expert_total, dtype=jnp.int32)[None, None, :]).astype(jnp.float32)
    chosen_logits = lax.optimization_barrier(jnp.sum(logits[:, None, :] * picked, axis=-1))
    first_gate = 1.0 / (1.0 + jnp.exp(chosen_logits[:, 1] - chosen_logits[:, 0]))
    second_gate = 1.0 / (1.0 + jnp.exp(chosen_logits[:, 0] - chosen_logits[:, 1]))
    return (first_gate, second_gate)

def layer(hidden, validity, chosen, gain_row, router_matrix, up_matrix, down_matrix, window):
    widened, normed = normalize(hidden, gain_row)
    first_gate, second_gate = gate_pair(normed, router_matrix, chosen)
    first_hit = (chosen[:, 0] == window).astype(jnp.float32)
    second_hit = (chosen[:, 1] == window).astype(jnp.float32)
    weight_gate = first_gate * first_hit + second_gate * second_hit
    live_hit = (first_hit + second_hit) * validity
    blocks = live_hit.reshape(-1, TOK_DEV)
    slot_index = (jnp.cumsum(blocks, axis=1) - blocks).reshape(-1).astype(jnp.int32)
    source = jnp.arange(TOKENS, dtype=jnp.int32) // TOK_DEV
    slot_total = TOKENS // TOK_DEV * CAP
    target = jnp.where(live_hit > 0.5, source * CAP + slot_index, slot_total)
    buffer = jnp.zeros((slot_total, D), jnp.bfloat16).at[target].set(normed, mode='drop')
    inner_sum = jnp.dot(buffer, up_matrix, preferred_element_type=jnp.float32)
    active = jax.nn.gelu(inner_sum).astype(jnp.bfloat16)
    group_count = TOKENS // TOK_DEV
    group_width = HID // group_count
    active_groups = jnp.transpose(active.reshape(slot_total, group_count, group_width), (1, 0, 2))
    down_groups = down_matrix.reshape(group_count, group_width, D)

    def add_group(total, pair):
        partial_sum = jnp.dot(pair[0], pair[1], preferred_element_type=jnp.float32)
        rounded = lax.optimization_barrier(partial_sum.astype(jnp.bfloat16))
        return (total + rounded.astype(jnp.float32), None)
    summed, _ = lax.scan(add_group, jnp.zeros((slot_total, D), jnp.float32), (active_groups, down_groups))
    expert_out = summed.astype(jnp.bfloat16)
    clipped = jnp.minimum(target, slot_total - 1)
    rows = jnp.take(expert_out, clipped, axis=0).astype(jnp.float32)
    mixture = (weight_gate * live_hit)[:, None] * rows
    return (widened + mixture).astype(jnp.bfloat16)

def apply_layer(packed):
    return layer(packed[0], packed[1], packed[2], packed[3], packed[4], packed[5], packed[6], packed[7])

def reference(stream, lengths, routes, norm_gains, router_weights, up_weights, down_weights):
    token_ids = jnp.arange(TOKENS, dtype=jnp.int32)
    owners = token_ids // SEQ
    offsets = token_ids % SEQ
    validity = (offsets[None, :] < lengths[:, owners]).astype(jnp.float32)
    windows = jnp.arange(SECTIONS, dtype=jnp.int32)
    first_tick = lax.map(apply_layer, (stream, validity, routes[0], norm_gains, router_weights, up_weights, down_weights, windows))
    second_tick = lax.map(apply_layer, (first_tick[:-1], validity[:-1], routes[1, 1:], norm_gains[1:], router_weights[1:], up_weights[1:], down_weights[1:], windows[1:]))
    return jnp.concatenate([first_tick[-1:], second_tick], axis=0)
```

```python
import functools

import jax
import jax.numpy as jnp
from jax import lax
from jax.experimental import pallas as pl
from jax.experimental.pallas import tpu as pltpu
from jax.sharding import PartitionSpec as P

MESH = pl.DeviceIdType.MESH
EPSILON = 1e-06
CAPACITY = 12

CHILDREN = {0: (2, 1), 2: (4, 3), 4: (6, 5), 6: (8, 7)}
STAGES = (((2,), (1,)), ((4,), (3,)), ((6,), (5,)), ((), (7, 8)))
PARENT = {child: node for node, kids in CHILDREN.items() for child in kids}
FAR = 8


def slot_order():
    order, groups = [(0, 1)], []
    for inner, leaves in STAGES:
        first = len(order) if groups else 0
        for node in inner + leaves:
            order += [(node, 1)] if node == FAR else [(node, 1), (node, -1)]
        groups.append((first, len(order)))
    places = {pair: place for place, pair in enumerate(order)}
    places[(FAR, -1)] = places[(FAR, 1)]
    places[(0, -1)] = 0
    return places, groups


PLACE, GROUPS = slot_order()
OFFSETS = sorted({sign * (child - node) for child, node in PARENT.items() for sign in (1, -1)})


def body(
    sizes,
    stream_ref, lengths_ref, routes_ref, gains_ref, router_ref, up_ref, down_ref,
    out_ref,
    held, held_prev, merged, info, info_prev, up_own, up_other, up_joint, down_all, router_all,
    gathered, unpacked, hidden, raw, packed_sums, outgoing, incoming, finished, finished_prev, staged,
    local_sem, swap_send, swap_recv, shift_send, shift_recv,
    gather_send, gather_recv, reduce_send, reduce_recv, out_sem,
):
    sections, ranks, rows, width, own_hidden = sizes
    main = width // 4 * 3
    part = main // 3
    half = 8 * 128
    wide = own_hidden // 256 * 256
    rest = own_hidden - wide
    section = lax.axis_index("section")
    rank = lax.axis_index("expert")
    chip, core = rank // 2, lax.rem(rank, 2)
    sibling = (section, rank + 1 - 2 * core)
    following = (lax.rem(section + 1, sections), rank)
    previous = (lax.rem(section + sections - 1, sections), rank)

    def along(steps):
        return (section, lax.rem(rank + 2 * steps + ranks, ranks))

    def columns(node, sign):
        if node != FAR:
            return pl.ds(0, main)
        return pl.ds(0, half) if sign > 0 else pl.ds(half, main - half)

    def remote(src, dst, send, recv, device):
        return pltpu.make_async_remote_copy(
            src_ref=src, dst_ref=dst, send_sem=send, recv_sem=recv, device_id=device, device_id_type=MESH
        )

    loads = [
        pltpu.make_async_copy(stream_ref.at[0], held, local_sem.at[0]),
        pltpu.make_async_copy(router_ref.at[0], router_all, local_sem.at[1]),
        pltpu.make_async_copy(up_ref.at[0], up_own, local_sem.at[2]),
        pltpu.make_async_copy(down_ref.at[0, pl.ds(0, wide)], down_all.at[pl.ds(0, wide)], local_sem.at[3]),
        pltpu.make_async_copy(
            down_ref.at[0, pl.ds(wide, rest)], down_all.at[pl.ds(2 * wide, rest)], local_sem.at[4]
        ),
    ]
    for load in loads:
        load.start()

    barrier = pltpu.get_barrier_semaphore()
    peers = [along(offset) for offset in OFFSETS] + [sibling, following, previous]
    for peer in peers:
        pl.semaphore_signal(barrier, inc=1, device_id=peer, device_id_type=MESH)

    lane = lax.broadcasted_iota(jnp.int32, (rows, rows), 1)
    row = lax.broadcasted_iota(jnp.int32, (rows, rows), 0)
    before = (row > lane).astype(jnp.bfloat16)
    slot_row = lax.broadcasted_iota(jnp.int32, (16, part), 0)
    gain = gains_ref[...].astype(jnp.float32)

    def pack(value):
        tail = value[:, main:]
        pieces = []
        for i in range(3):
            moved = pltpu.roll(tail, 12 - 4 * i, 0)
            pieces.append(jnp.where(slot_row < CAPACITY, value[:, i * part : (i + 1) * part], moved))
        return pieces

    def tail_of(pieces):
        result = pltpu.roll(pieces[0], 4, 0)
        result = jnp.where(slot_row < 4, result, pltpu.roll(pieces[1], 8, 0))
        result = jnp.where(slot_row < 8, result, pltpu.roll(pieces[2], 12, 0))
        return result

    def placing(chosen, validity):
        first = jnp.broadcast_to(chosen[:, 0:1], (rows, rows))
        second = jnp.broadcast_to(chosen[:, 1:2], (rows, rows))
        hit = ((first == section) | (second == section)).astype(jnp.float32) * validity
        slot = jnp.dot(before, hit.astype(jnp.bfloat16), preferred_element_type=jnp.float32)
        spread = jnp.where((slot == lane.astype(jnp.float32)) & (hit > 0.5), 1.0, 0.0)
        return first, second, hit, spread, jnp.transpose(spread)

    def normalize(x):
        mean_square = jnp.sum(x * x, axis=-1, keepdims=True) * (1.0 / width)
        return x * lax.rsqrt(mean_square + EPSILON) * gain

    def gates(normed, picking, first, second):
        logits = jnp.dot(normed, router_all[...], preferred_element_type=jnp.float32)
        experts = logits.shape[1]
        ids = lax.broadcasted_iota(jnp.int32, logits.shape, 1).astype(jnp.float32)
        chosen = [
            jnp.dot(picking, q.astype(jnp.float32).astype(jnp.bfloat16), preferred_element_type=jnp.float32)[:, :experts]
            for q in (first, second)
        ]
        a, b = (jnp.sum(jnp.where(ids == q, logits, 0.0), axis=-1, keepdims=True) for q in chosen)
        first_gate = 1.0 / (1.0 + jnp.exp(b - a))
        second_gate = 1.0 / (1.0 + jnp.exp(a - b))
        mine = section.astype(jnp.float32)
        return jnp.where(
            chosen[0][:, 0:1] == mine, first_gate, jnp.where(chosen[1][:, 0:1] == mine, second_gate, 0.0)
        )

    def gather_copy(tick, node, child, sign):
        cols = columns(child, sign)
        way = 0 if sign > 0 else 1
        return remote(
            gathered.at[tick, PLACE[(node, sign)], :, cols],
            gathered.at[tick, PLACE[(child, sign)], :, cols],
            gather_send.at[tick, way, child],
            gather_recv.at[tick, way, child],
            along(sign * (child - node)),
        )

    def reduce_copy(tick, child, sign):
        cols = columns(child, sign)
        way = 0 if sign > 0 else 1
        return remote(
            outgoing.at[tick, way, child, :, cols],
            incoming.at[tick, way, child, :, cols],
            reduce_send.at[tick, way, child],
            reduce_recv.at[tick, way, child],
            along(sign * (child - PARENT[child])),
        )

    def forward(tick, node):
        for child in CHILDREN.get(node, ()):
            for sign in (1, -1):
                gather_copy(tick, node, child, sign).start()

    def expert(tick, first, last):
        low, count = 16 * first, 16 * (last - first)
        for place in range(first, last):
            at = pl.ds(16 * place, 16)
            block = gathered[tick, place]
            unpacked[at, 0:main] = block
            wider = block.astype(jnp.float32)
            tail = tail_of([wider[:, i * part : (i + 1) * part] for i in range(3)])
            unpacked[at, main:width] = tail.astype(jnp.bfloat16)
        at = pl.ds(low, count)
        tokens = unpacked[at, :]
        for begin, matrix in ((0, up_own[:, 0:wide]), (wide, up_other[:, 0:wide]), (2 * wide, up_joint[...])):
            inner = jnp.dot(tokens, matrix, preferred_element_type=jnp.float32)
            hidden[at, begin : begin + inner.shape[1]] = jax.nn.gelu(inner).astype(jnp.bfloat16)
        active = hidden[at, :]
        for begin in range(0, width, 512):
            raw[at, begin : begin + 512] = jnp.dot(
                active, down_all[:, begin : begin + 512], preferred_element_type=jnp.float32
            )
        for place in range(first, last):
            for i, piece in enumerate(pack(raw[pl.ds(16 * place, 16), :])):
                packed_sums[place, :, i * part : (i + 1) * part] = piece

    def send_sum(tick, node, sign):
        way = 0 if sign > 0 else 1
        cols = columns(node, sign)
        for child in CHILDREN.get(node, ()):
            reduce_copy(tick, child, sign).wait_recv()
        if FAR in CHILDREN.get(node, ()):
            other = [child for child in CHILDREN[node] if child != FAR]
            for near, far_cols in ((True, columns(FAR, sign)), (False, columns(FAR, -sign))):
                value = packed_sums[PLACE[(node, -sign)], :, far_cols]
                for child in other + ([FAR] if near else []):
                    value = value + incoming[tick, way, child, :, far_cols].astype(jnp.float32)
                outgoing[tick, way, node, :, far_cols] = value.astype(jnp.bfloat16)
        else:
            total = packed_sums[PLACE[(node, -sign)], :, cols]
            for child in CHILDREN.get(node, ()):
                total = total + incoming[tick, way, child, :, cols].astype(jnp.float32)
            outgoing[tick, way, node, :, cols] = total.astype(jnp.bfloat16)
        reduce_copy(tick, node, sign).start()

    def mixture(tick, normed, meanwhile, weights_ready=None):
        for i, piece in enumerate(pack(normed)):
            gathered[tick, 0, :, i * part : (i + 1) * part] = piece.astype(jnp.bfloat16)
        forward(tick, 0)
        meanwhile()
        for (inner, leaves), (first, last) in zip(STAGES, GROUPS):
            for node in inner:
                for sign in (1, -1):
                    gather_copy(tick, PARENT[node], node, sign).wait_recv()
                forward(tick, node)
            for node in leaves:
                for sign in (1, -1):
                    gather_copy(tick, PARENT[node], node, sign).wait_recv()
            if first == 0 and weights_ready:
                weights_ready()
            expert(tick, first, last)
            for node in leaves:
                for sign in (1, -1):
                    send_sum(tick, node, sign)
        for inner, _ in reversed(STAGES):
            for node in inner:
                for sign in (1, -1):
                    send_sum(tick, node, sign)
        total = packed_sums[0]
        for child in CHILDREN[0]:
            for sign in (1, -1):
                reduce_copy(tick, child, sign).wait_recv()
        for child in CHILDREN[0]:
            for way in (0, 1):
                total = total + incoming[tick, way, child].astype(jnp.float32)
        pieces = [total[:, i * part : (i + 1) * part] for i in range(3)]
        keep = slot_row < CAPACITY
        summed = jnp.concatenate([jnp.where(keep, p, 0.0) for p in pieces] + [jnp.where(keep, tail_of(pieces), 0.0)], axis=1)
        return summed.astype(jnp.bfloat16).astype(jnp.float32)

    own_length = lengths_ref[0, chip]
    validity = ((core * rows + row) < own_length).astype(jnp.float32)
    first, second, _, spread, picked = placing(routes_ref[0, 0], validity)
    info[...] = jnp.where(lane < 16, spread, validity).astype(jnp.bfloat16)
    picking = picked[0:16].astype(jnp.bfloat16)
    loads[0].wait()
    x = jnp.dot(picking, held[...], preferred_element_type=jnp.float32)
    normed = normalize(x).astype(jnp.bfloat16)
    pl.semaphore_wait(barrier, len(peers))

    swaps = [
        remote(up_ref.at[0], up_other, swap_send.at[0], swap_recv.at[0], sibling),
        remote(
            down_ref.at[0, pl.ds(0, wide)], down_all.at[pl.ds(wide, wide)], swap_send.at[1], swap_recv.at[1], sibling
        ),
        remote(
            down_ref.at[0, pl.ds(wide, rest)],
            down_all.at[pl.ds(2 * wide + rest, rest)],
            swap_send.at[2],
            swap_recv.at[2],
            sibling,
        ),
    ]
    shifts = [
        remote(info, info_prev, shift_send.at[0], shift_recv.at[0], following),
        remote(stream_ref.at[0], held_prev, shift_send.at[1], shift_recv.at[1], following),
        remote(finished, finished_prev, shift_send.at[2], shift_recv.at[2], following),
    ]
    gate = [None, None]

    def first_meanwhile():
        for copy in swaps + shifts[:2]:
            copy.start()
        loads[1].wait()
        gate[0] = gates(normed, picking, first, second)

    def weights_ready():
        for load in loads[2:]:
            load.wait()
        for copy in swaps:
            copy.wait_recv()
        up_joint[...] = jnp.concatenate([up_own[:, wide:], up_other[:, wide:]], axis=1)

    summed = mixture(0, normed.astype(jnp.float32), first_meanwhile, weights_ready)
    for i, piece in enumerate(pack(x + gate[0] * summed)):
        finished[:, i * part : (i + 1) * part] = piece.astype(jnp.bfloat16)
    shifts[2].start()

    shifts[0].wait_recv()
    prior = info_prev[...].astype(jnp.float32)
    live = jnp.broadcast_to(prior[:, 64:65], (rows, rows)) * (section != 0).astype(jnp.float32)
    prior_spread = jnp.where(lane < 16, prior, 0.0)
    prior_picked = jnp.transpose(prior_spread)
    renewed_row = jnp.sum(prior_picked, axis=0, keepdims=True)
    renewed = jnp.sum(prior_spread, axis=1, keepdims=True)
    first2, second2, hit2, spread2, picked2 = placing(routes_ref[1, 0], live)
    picking2 = picked2[0:16].astype(jnp.bfloat16)
    old_rows = (picked2[0:16] * (1.0 - renewed_row)).astype(jnp.bfloat16)
    new_rows = jnp.dot(picking2, prior_spread.astype(jnp.bfloat16), preferred_element_type=jnp.float32)
    new_rows = new_rows[:, 0:16].astype(jnp.bfloat16)
    shifts[1].wait_recv()
    kept = jnp.dot(old_rows, held_prev[...], preferred_element_type=jnp.float32)

    shifts[2].wait_recv()
    block = finished_prev[...].astype(jnp.float32)
    pieces = [block[:, i * part : (i + 1) * part] for i in range(3)]
    keep = slot_row < CAPACITY
    update = jnp.concatenate(
        [jnp.where(keep, p, 0.0) for p in pieces] + [jnp.where(keep, tail_of(pieces), 0.0)], axis=1
    ).astype(jnp.bfloat16)
    x2 = kept + jnp.dot(new_rows, update, preferred_element_type=jnp.float32)
    normed2 = normalize(x2).astype(jnp.bfloat16)

    def second_meanwhile():
        gate[1] = gates(normed2, picking2, first2, second2)
        placed = jnp.dot(
            prior_spread[:, 0:16].astype(jnp.bfloat16), update, preferred_element_type=jnp.float32
        ).astype(jnp.bfloat16)
        merged[...] = jnp.where(renewed > 0.5, placed, held_prev[...])

    summed2 = mixture(1, normed2.astype(jnp.float32), second_meanwhile)
    final = (x2 + gate[1] * summed2).astype(jnp.bfloat16)
    spread_final = spread2[:, 0:16].astype(jnp.bfloat16)
    struck = hit2[:, 0:1] > 0.5
    stores = []
    for i in range(4):
        cols = pl.ds(i * part, part)
        placed = jnp.dot(spread_final, final[:, i * part : (i + 1) * part], preferred_element_type=jnp.float32)
        staged[:, cols] = jnp.where(struck, placed.astype(jnp.bfloat16), merged[:, cols])
        store = pltpu.make_async_copy(staged.at[:, cols], out_ref.at[0, :, cols], out_sem.at[i])
        store.start()
        stores.append(store)
    for tick in (0, 1):
        for child in PARENT:
            for sign in (1, -1):
                gather_copy(tick, PARENT[child], child, sign).wait_send()
                reduce_copy(tick, child, sign).wait_send()
    for copy in swaps + shifts:
        copy.wait_send()
    for store in stores:
        store.wait()


def shards(stream, lengths, routes, norm_gains, router_weights, up_weights, down_weights):
    rows, width = stream.shape[1:]
    own_hidden = up_weights.shape[2]
    experts = router_weights.shape[2]
    main = width // 4 * 3
    sizes = (lax.axis_size("section"), lax.axis_size("expert"), rows, width, own_hidden)
    bf16, f32 = jnp.bfloat16, jnp.float32
    anywhere = pl.BlockSpec(memory_space=pl.ANY)
    vmem = pl.BlockSpec(memory_space=pltpu.VMEM)
    dma = pltpu.SemaphoreType.DMA
    return pl.pallas_call(
        functools.partial(body, sizes),
        out_shape=jax.ShapeDtypeStruct(stream.shape, bf16),
        in_specs=[anywhere, pl.BlockSpec(memory_space=pltpu.SMEM), vmem, vmem, anywhere, anywhere, anywhere],
        out_specs=anywhere,
        scratch_shapes=[
            pltpu.VMEM((rows, width), bf16),
            pltpu.VMEM((rows, width), bf16),
            pltpu.VMEM((rows, width), bf16),
            pltpu.VMEM((rows, rows), bf16),
            pltpu.VMEM((rows, rows), bf16),
            pltpu.VMEM((width, own_hidden), bf16),
            pltpu.VMEM((width, own_hidden), bf16),
            pltpu.VMEM((width, 128), bf16),
            pltpu.VMEM((2 * own_hidden, width), bf16),
            pltpu.VMEM((width, experts), bf16),
            pltpu.VMEM((2, 16, 16, main), bf16),
            pltpu.VMEM((256, width), bf16),
            pltpu.VMEM((256, 2 * own_hidden), bf16),
            pltpu.VMEM((256, width), f32),
            pltpu.VMEM((16, 16, main), f32),
            pltpu.VMEM((2, 2, 9, 16, main), bf16),
            pltpu.VMEM((2, 2, 9, 16, main), bf16),
            pltpu.VMEM((16, main), bf16),
            pltpu.VMEM((16, main), bf16),
            pltpu.VMEM((rows, width), bf16),
            dma((5,)),
            dma((3,)),
            dma((3,)),
            dma((3,)),
            dma((3,)),
            dma((2, 2, 9)),
            dma((2, 2, 9)),
            dma((2, 2, 9)),
            dma((2, 2, 9)),
            dma((4,)),
        ],
        compiler_params=pltpu.CompilerParams(
            collective_id=0, has_side_effects=True, vmem_limit_bytes=48 * 1024 * 1024
        ),
    )(stream, lengths, routes, norm_gains, router_weights, up_weights, down_weights)


def solution(mesh):
    in_specs = (
        P("section", "expert", None),
        P("section", None),
        P(None, "section", "expert", None),
        P("section", None),
        P("section", None, None),
        P("section", None, "expert"),
        P("section", "expert", None),
    )
    out_specs = P("section", "expert", None)
    return jax.shard_map(shards, mesh=mesh, in_specs=in_specs, out_specs=out_specs, check_vma=False)
```

```python
import functools

import jax
import jax.numpy as jnp
from jax import lax
from jax.experimental import pallas as pl
from jax.experimental.pallas import tpu as pltpu
from jax.sharding import PartitionSpec as P

MESH = pl.DeviceIdType.MESH
EPSILON = 1e-06
CAPACITY = 12
VMEM_LIMIT = 60 * 1024 * 1024

CHILDREN = {0: (3, 1), 3: (6, 4, 2), 6: (8, 7, 5)}
STAGES = (((3,), (1,)), ((6,), (4, 2)), ((), (8, 7, 5)))
PARENT = {child: node for node, kids in CHILDREN.items() for child in kids}
FAR = 8


def slot_order():
    order, groups = [(0, 1)], []
    for inner, leaves in STAGES:
        first = len(order) if groups else 0
        for node in inner + leaves:
            order += [(node, 1)] if node == FAR else [(node, 1), (node, -1)]
        groups.append((first, len(order)))
    places = {pair: place for place, pair in enumerate(order)}
    places[(FAR, -1)] = places[(FAR, 1)]
    places[(0, -1)] = 0
    return places, groups


PLACE, GROUPS = slot_order()
PIECES = 3


def travels(node, sign, piece):
    return node != FAR or (piece < 2) == (sign > 0)


OFFSETS = sorted({sign * (child - node) for child, node in PARENT.items() for sign in (1, -1)})


def body(
    sizes,
    stream_ref, lengths_ref, routes_ref, gains_ref, router_ref, up_ref, down_ref,
    out_ref,
    held, held_prev, merged, info, info_prev, up_all, down_all, router_all,
    gathered, unpacked, hidden, raw, packed_sums, outgoing, incoming, own_sum, own_prev, gate_out, gate_prev, staged,
    local_sem, swap_send, swap_recv, shift_send, shift_recv,
    gather_send, gather_recv, reduce_send, reduce_recv, out_sem,
):
    sections, ranks, rows, width, own_hidden = sizes
    main = width // 4 * 3
    part = main // 3
    mine, theirs = pl.ds(0, own_hidden), pl.ds(own_hidden, own_hidden)
    section = lax.axis_index("section")
    rank = lax.axis_index("expert")
    chip, core = rank // 2, lax.rem(rank, 2)
    sibling = (section, rank + 1 - 2 * core)
    following = (lax.rem(section + 1, sections), rank)
    previous = (lax.rem(section + sections - 1, sections), rank)

    def along(steps):
        return (section, lax.rem(rank + 2 * steps + ranks, ranks))

    def onward(steps):
        return (following[0], lax.rem(rank + 2 * steps + ranks, ranks))

    def backward(steps):
        return (previous[0], lax.rem(rank + 2 * steps + ranks, ranks))

    columns = [pl.ds(i * part, part) for i in range(PIECES)]

    def remote(src, dst, send, recv, device):
        return pltpu.make_async_remote_copy(
            src_ref=src, dst_ref=dst, send_sem=send, recv_sem=recv, device_id=device, device_id_type=MESH
        )

    loads = [
        pltpu.make_async_copy(stream_ref.at[0], held, local_sem.at[0]),
        pltpu.make_async_copy(router_ref.at[0], router_all, local_sem.at[1]),
        pltpu.make_async_copy(up_ref.at[0], up_all.at[mine], local_sem.at[2]),
        pltpu.make_async_copy(down_ref.at[0], down_all.at[mine], local_sem.at[3]),
    ]
    for load in loads:
        load.start()

    barrier = pltpu.get_barrier_semaphore()
    last_hops = sorted({sign * child for child in CHILDREN[0] for sign in (1, -1)}) + [0]
    peers = [along(offset) for offset in OFFSETS] + [sibling]
    peers += [place(offset) for place in (onward, backward) for offset in last_hops]
    for peer in peers:
        pl.semaphore_signal(barrier, inc=1, device_id=peer, device_id_type=MESH)

    lane = lax.broadcasted_iota(jnp.int32, (rows, rows), 1)
    row = lax.broadcasted_iota(jnp.int32, (rows, rows), 0)
    before = (row < lane).astype(jnp.bfloat16)
    slot_row = lax.broadcasted_iota(jnp.int32, (16, part), 0)
    gain = gains_ref[...].astype(jnp.float32)

    def pack(value):
        tail = value[:, main:]
        pieces = []
        for i in range(3):
            moved = pltpu.roll(tail, 12 - 4 * i, 0)
            pieces.append(jnp.where(slot_row < CAPACITY, value[:, i * part : (i + 1) * part], moved))
        return pieces

    def tail_of(pieces):
        result = pltpu.roll(pieces[0], 4, 0)
        result = jnp.where(slot_row < 4, result, pltpu.roll(pieces[1], 8, 0))
        result = jnp.where(slot_row < 8, result, pltpu.roll(pieces[2], 12, 0))
        return result

    def placing(first, second, validity):
        hit = ((first == section) | (second == section)).astype(jnp.float32) * validity
        hit = jnp.broadcast_to(hit, (rows, rows))
        slot = jnp.dot(hit.astype(jnp.bfloat16), before, preferred_element_type=jnp.float32)
        return jnp.where((slot == row.astype(jnp.float32)) & (hit > 0.5), 1.0, 0.0)

    def normalize(x):
        mean_square = jnp.sum(x * x, axis=-1, keepdims=True) * (1.0 / width)
        return x * lax.rsqrt(mean_square + EPSILON) * gain

    def gates(normed, picked, first, second):
        logits = lax.dot_general(
            normed, router_all[...], (((1,), (1,)), ((), ())), preferred_element_type=jnp.float32
        )
        ids = lax.broadcasted_iota(jnp.int32, logits.shape, 1).astype(jnp.float32)
        chosen = [jnp.sum(picked * q.astype(jnp.float32), axis=1, keepdims=True) for q in (first, second)]
        a, b = (jnp.sum(jnp.where(ids == q, logits, 0.0), axis=-1, keepdims=True) for q in chosen)
        first_gate = 1.0 / (1.0 + jnp.exp(b - a))
        second_gate = 1.0 / (1.0 + jnp.exp(a - b))
        window = section.astype(jnp.float32)
        return jnp.where(chosen[0] == window, first_gate, jnp.where(chosen[1] == window, second_gate, 0.0))

    def gather_copy(tick, node, child, sign, piece):
        cols = columns[piece]
        way = 0 if sign > 0 else 1
        return remote(
            gathered.at[tick, PLACE[(node, sign)], :, cols],
            gathered.at[tick, PLACE[(child, sign)], :, cols],
            gather_send.at[tick, way, child, piece],
            gather_recv.at[tick, way, child, piece],
            along(sign * (child - node)),
        )

    def reduce_copy(tick, child, sign, piece):
        cols = columns[piece]
        way = 0 if sign > 0 else 1
        steps = sign * (child - PARENT[child])
        return remote(
            outgoing.at[tick, way, child, :, cols],
            incoming.at[tick, way, child, :, cols],
            reduce_send.at[tick, way, child, piece],
            reduce_recv.at[tick, way, child, piece],
            onward(steps) if tick == 0 and PARENT[child] == 0 else along(steps),
        )

    def both(node):
        return [(piece, sign) for piece in range(PIECES) for sign in (1, -1) if travels(node, sign, piece)]

    def arrive(tick, node, pass_on):
        for piece, sign in both(node):
            gather_copy(tick, PARENT[node], node, sign, piece).wait_recv()
            if pass_on:
                forward(tick, node, piece, sign)

    def forward(tick, node, piece, sign):
        for child in CHILDREN[node]:
            if child in CHILDREN:
                gather_copy(tick, node, child, sign, piece).start()

    def forward_leaves(tick, node):
        for child in CHILDREN[node]:
            if child not in CHILDREN:
                for piece, sign in both(child):
                    gather_copy(tick, node, child, sign, piece).start()

    def expert(tick, first, last):
        low, count = 16 * first, 16 * (last - first)
        for place in range(first, last):
            at = pl.ds(16 * place, 16)
            block = gathered[tick, place]
            unpacked[at, 0:main] = block
            wider = block.astype(jnp.float32)
            tail = tail_of([wider[:, i * part : (i + 1) * part] for i in range(3)])
            unpacked[at, main:width] = tail.astype(jnp.bfloat16)
        at = pl.ds(low, count)
        tokens = unpacked[at, :]
        for begin in range(0, 2 * own_hidden, 256):
            end = min(begin + 256, 2 * own_hidden)
            inner = lax.dot_general(
                tokens, up_all[begin:end, :], (((1,), (1,)), ((), ())), preferred_element_type=jnp.float32
            )
            hidden[at, begin:end] = jax.nn.gelu(inner).astype(jnp.bfloat16)
        active = hidden[at, :]
        for begin in range(0, width, 512):
            raw[at, begin : begin + 512] = jnp.dot(
                active, down_all[:, begin : begin + 512], preferred_element_type=jnp.float32
            )
        for place in range(first, last):
            for i, piece in enumerate(pack(raw[pl.ds(16 * place, 16), :])):
                packed_sums[place, :, i * part : (i + 1) * part] = piece

    def send_sum(tick, node):
        for piece, sign in both(node):
            way = 0 if sign > 0 else 1
            cols = columns[piece]
            total = packed_sums[PLACE[(node, -sign)], :, cols]
            for child in CHILDREN.get(node, ()):
                if travels(child, sign, piece):
                    reduce_copy(tick, child, sign, piece).wait_recv()
                    total = total + incoming[tick, way, child, :, cols].astype(jnp.float32)
            outgoing[tick, way, node, :, cols] = total.astype(jnp.bfloat16)
            reduce_copy(tick, node, sign, piece).start()

    def spread_and_sum(tick, normed, meanwhile, weights_ready=None, first_done=None):
        for i, piece in enumerate(pack(normed)):
            gathered[tick, 0, :, i * part : (i + 1) * part] = piece.astype(jnp.bfloat16)
        for piece, sign in both(0):
            forward(tick, 0, piece, sign)
        forward_leaves(tick, 0)
        meanwhile()
        for (inner, leaves), (first, last) in zip(STAGES, GROUPS):
            for node in inner:
                arrive(tick, node, True)
                forward_leaves(tick, node)
            for node in leaves:
                arrive(tick, node, False)
            if first == 0 and weights_ready:
                weights_ready()
            expert(tick, first, last)
            if first == 0 and first_done:
                first_done()
            for node in leaves:
                send_sum(tick, node)
        for inner, _ in reversed(STAGES):
            for node in inner:
                send_sum(tick, node)

    def summed(tick, own):
        pieces = []
        for piece in range(PIECES):
            total = own[:, piece * part : (piece + 1) * part].astype(jnp.float32)
            for child in CHILDREN[0]:
                for sign in (1, -1):
                    reduce_copy(tick, child, sign, piece).wait_recv()
                    way = 0 if sign > 0 else 1
                    total = total + incoming[tick, way, child, :, columns[piece]].astype(jnp.float32)
            pieces.append(total)
        keep = slot_row < CAPACITY
        whole = [jnp.where(keep, p, 0.0) for p in pieces + [tail_of(pieces)]]
        return jnp.concatenate(whole, axis=1).astype(jnp.bfloat16).astype(jnp.float32)

    own_length = lengths_ref[0, chip]
    position = core * rows + lane[0:1]
    validity = (position < own_length).astype(jnp.float32)
    first, second = routes_ref[0, 0, 0:1], routes_ref[0, 0, 1:2]
    picked = placing(first, second, validity)
    info[...] = jnp.where(row < 16, picked, validity).astype(jnp.bfloat16)
    picked = picked[0:16]
    loads[0].wait()
    x = jnp.dot(picked.astype(jnp.bfloat16), held[...], preferred_element_type=jnp.float32)
    normed = normalize(x).astype(jnp.bfloat16)
    pl.semaphore_wait(barrier, len(peers))

    swaps = [
        remote(up_ref.at[0], up_all.at[theirs], swap_send.at[0], swap_recv.at[0], sibling),
        remote(down_ref.at[0], down_all.at[theirs], swap_send.at[1], swap_recv.at[1], sibling),
    ]
    shifts = [
        remote(info, info_prev, shift_send.at[0], shift_recv.at[0], following),
        remote(stream_ref.at[0], held_prev, shift_send.at[1], shift_recv.at[1], following),
        remote(gate_out, gate_prev, shift_send.at[2], shift_recv.at[2], following),
        remote(own_sum, own_prev, shift_send.at[3], shift_recv.at[3], following),
    ]
    def first_meanwhile():
        for copy in swaps + shifts[:2]:
            copy.start()
        loads[1].wait()
        gate_out[...] = jnp.broadcast_to(gates(normed, picked, first, second), gate_out.shape)
        shifts[2].start()

    def first_done():
        own_sum[...] = packed_sums[0].astype(jnp.bfloat16)
        shifts[3].start()

    def weights_ready():
        for load in loads[2:]:
            load.wait()
        for copy in swaps:
            copy.wait_recv()

    spread_and_sum(0, normed.astype(jnp.float32), first_meanwhile, weights_ready, first_done)

    shifts[0].wait_recv()
    prior = info_prev[...].astype(jnp.float32)
    live = prior[64:65] * (section != 0).astype(jnp.float32)
    prior_picked = jnp.where(row < 16, prior, 0.0)
    prior_spread = jnp.transpose(prior_picked)
    renewed_row = jnp.sum(prior_picked, axis=0, keepdims=True)
    renewed = jnp.sum(prior_spread, axis=1, keepdims=True)
    first2, second2 = routes_ref[1, 0, 0:1], routes_ref[1, 0, 1:2]
    picked2 = placing(first2, second2, live)
    spread2 = jnp.transpose(picked2)
    hit2 = jnp.sum(spread2, axis=1, keepdims=True)
    picked2 = picked2[0:16]
    old_rows = (picked2 * (1.0 - renewed_row)).astype(jnp.bfloat16)
    new_rows = jnp.dot(
        picked2.astype(jnp.bfloat16), prior_spread.astype(jnp.bfloat16), preferred_element_type=jnp.float32
    )
    new_rows = new_rows[:, 0:16].astype(jnp.bfloat16)
    shifts[1].wait_recv()
    kept = jnp.dot(old_rows, held_prev[...], preferred_element_type=jnp.float32)

    prior_x = jnp.dot(prior_picked[0:16].astype(jnp.bfloat16), held_prev[...], preferred_element_type=jnp.float32)
    shifts[2].wait_recv()
    prior_gate = gate_prev[:, 0:1]
    shifts[3].wait_recv()
    update = (prior_x + prior_gate * summed(0, own_prev)).astype(jnp.bfloat16)
    x2 = kept + jnp.dot(new_rows, update, preferred_element_type=jnp.float32)
    normed2 = normalize(x2).astype(jnp.bfloat16)

    gate = []

    def second_meanwhile():
        gate.append(gates(normed2, picked2, first2, second2))
        placed = jnp.dot(
            prior_spread[:, 0:16].astype(jnp.bfloat16), update, preferred_element_type=jnp.float32
        ).astype(jnp.bfloat16)
        merged[...] = jnp.where(renewed > 0.5, placed, held_prev[...])

    spread_and_sum(1, normed2.astype(jnp.float32), second_meanwhile)
    final = (x2 + gate[0] * summed(1, packed_sums.at[0])).astype(jnp.bfloat16)
    spread_final = spread2[:, 0:16].astype(jnp.bfloat16)
    struck = hit2 > 0.5
    stores = []
    for i in range(4):
        cols = pl.ds(i * part, part)
        placed = jnp.dot(spread_final, final[:, i * part : (i + 1) * part], preferred_element_type=jnp.float32)
        staged[:, cols] = jnp.where(struck, placed.astype(jnp.bfloat16), merged[:, cols])
        store = pltpu.make_async_copy(staged.at[:, cols], out_ref.at[0, :, cols], out_sem.at[i])
        store.start()
        stores.append(store)
    for tick in (0, 1):
        for child in PARENT:
            for piece, sign in both(child):
                gather_copy(tick, PARENT[child], child, sign, piece).wait_send()
                reduce_copy(tick, child, sign, piece).wait_send()
    for copy in swaps + shifts:
        copy.wait_send()
    for store in stores:
        store.wait()


def shards(stream, lengths, routes, norm_gains, router_weights, up_weights, down_weights):
    rows, width = stream.shape[1:]
    own_hidden = up_weights.shape[2]
    experts = router_weights.shape[2]
    main = width // 4 * 3
    sizes = (lax.axis_size("section"), lax.axis_size("expert"), rows, width, own_hidden)
    bf16, f32 = jnp.bfloat16, jnp.float32
    anywhere = pl.BlockSpec(memory_space=pl.ANY)
    vmem = pl.BlockSpec(memory_space=pltpu.VMEM)
    dma = pltpu.SemaphoreType.DMA
    return pl.pallas_call(
        functools.partial(body, sizes),
        out_shape=jax.ShapeDtypeStruct(stream.shape, bf16),
        in_specs=[anywhere, pl.BlockSpec(memory_space=pltpu.SMEM), vmem, vmem, anywhere, anywhere, anywhere],
        out_specs=anywhere,
        scratch_shapes=[
            pltpu.VMEM((rows, width), bf16),
            pltpu.VMEM((rows, width), bf16),
            pltpu.VMEM((rows, width), bf16),
            pltpu.VMEM((rows, rows), bf16),
            pltpu.VMEM((rows, rows), bf16),
            pltpu.VMEM((2 * own_hidden, width), bf16),
            pltpu.VMEM((2 * own_hidden, width), bf16),
            pltpu.VMEM((experts, width), bf16),
            pltpu.VMEM((2, 16, 16, main), bf16),
            pltpu.VMEM((256, width), bf16),
            pltpu.VMEM((256, 2 * own_hidden), bf16),
            pltpu.VMEM((256, width), f32),
            pltpu.VMEM((16, 16, main), f32),
            pltpu.VMEM((2, 2, 9, 16, main), bf16),
            pltpu.VMEM((2, 2, 9, 16, main), bf16),
            pltpu.VMEM((16, main), bf16),
            pltpu.VMEM((16, main), bf16),
            pltpu.VMEM((16, 128), f32),
            pltpu.VMEM((16, 128), f32),
            pltpu.VMEM((rows, width), bf16),
            dma((4,)),
            dma((2,)),
            dma((2,)),
            dma((4,)),
            dma((4,)),
            dma((2, 2, 9, PIECES)),
            dma((2, 2, 9, PIECES)),
            dma((2, 2, 9, PIECES)),
            dma((2, 2, 9, PIECES)),
            dma((4,)),
        ],
        compiler_params=pltpu.CompilerParams(
            collective_id=0, has_side_effects=True, vmem_limit_bytes=VMEM_LIMIT
        ),
    )(
        stream,
        lengths,
        jnp.swapaxes(routes, 2, 3),
        norm_gains,
        jnp.swapaxes(router_weights, 1, 2),
        jnp.swapaxes(up_weights, 1, 2),
        down_weights,
    )


def solution(mesh):
    in_specs = (
        P("section", "expert", None),
        P("section", None),
        P(None, "section", "expert", None),
        P("section", None),
        P("section", None, None),
        P("section", None, "expert"),
        P("section", "expert", None),
    )
    out_specs = P("section", "expert", None)
    return jax.shard_map(shards, mesh=mesh, in_specs=in_specs, out_specs=out_specs, check_vma=False)
```

```python
import functools

import jax
import jax.numpy as jnp
from jax import lax
from jax.experimental import pallas as pl
from jax.experimental.pallas import tpu as pltpu
from jax.sharding import PartitionSpec as P

MESH = pl.DeviceIdType.MESH
EPSILON = 1e-06
CAPACITY = 12
VMEM_LIMIT = 60 * 1024 * 1024

CHILDREN = {0: (3, 1), 3: (6, 4, 2), 6: (8, 7, 5)}
STAGES = (((3,), (1,)), ((6,), (4, 2)), ((), (8, 7, 5)))
PARENT = {child: node for node, kids in CHILDREN.items() for child in kids}
FAR = 8
EAGER = (6,)


def slot_order():
    order, groups = [(0, 1)], []
    for inner, leaves in STAGES:
        first = len(order) if groups else 0
        for node in inner + leaves:
            order += [(node, 1)] if node == FAR else [(node, 1), (node, -1)]
        groups.append((first, len(order)))
    places = {pair: place for place, pair in enumerate(order)}
    places[(FAR, -1)] = places[(FAR, 1)]
    places[(0, -1)] = 0
    return places, groups


PLACE, GROUPS = slot_order()
PIECES = 3


def travels(node, sign, piece):
    return node != FAR or (piece < 2) == (sign > 0)


OFFSETS = sorted({sign * (child - node) for child, node in PARENT.items() for sign in (1, -1)})


def body(
    sizes,
    stream_ref, lengths_ref, routes_ref, gains_ref, router_ref, up_ref, down_ref,
    out_ref,
    held, held_prev, merged, info, info_prev, up_all, down_all, router_all,
    gathered, unpacked, hidden, raw, packed_sums, outgoing, incoming, own_sum, own_prev, gate_out, gate_prev, staged,
    local_sem, swap_send, swap_recv, shift_send, shift_recv,
    gather_send, gather_recv, reduce_send, reduce_recv, out_sem,
):
    sections, ranks, rows, width, own_hidden = sizes
    main = width // 4 * 3
    part = main // 3
    mine, theirs = pl.ds(0, own_hidden), pl.ds(own_hidden, own_hidden)
    section = lax.axis_index("section")
    rank = lax.axis_index("expert")
    chip, core = rank // 2, lax.rem(rank, 2)
    sibling = (section, rank + 1 - 2 * core)
    forth = 2 - 4 * core
    following = (lax.rem(section + 1, sections), rank)
    previous = (lax.rem(section + sections - 1, sections), rank)

    def along(steps):
        return (section, lax.rem(rank + forth * steps + ranks, ranks))

    def onward(steps):
        return (following[0], lax.rem(rank + forth * steps + ranks, ranks))

    def backward(steps):
        return (previous[0], lax.rem(rank + forth * steps + ranks, ranks))

    columns = [pl.ds(i * part, part) for i in range(PIECES)]

    def remote(src, dst, send, recv, device):
        return pltpu.make_async_remote_copy(
            src_ref=src, dst_ref=dst, send_sem=send, recv_sem=recv, device_id=device, device_id_type=MESH
        )

    loads = [
        pltpu.make_async_copy(stream_ref.at[0], held, local_sem.at[0]),
        pltpu.make_async_copy(router_ref.at[0], router_all, local_sem.at[1]),
        pltpu.make_async_copy(up_ref.at[0], up_all.at[mine], local_sem.at[2]),
        pltpu.make_async_copy(down_ref.at[0], down_all.at[mine], local_sem.at[3]),
    ]
    for load in loads:
        load.start()

    barrier = pltpu.get_barrier_semaphore()
    last_hops = sorted({sign * child for child in CHILDREN[0] for sign in (1, -1)}) + [0]
    peers = [along(offset) for offset in OFFSETS] + [sibling]
    peers += [place(offset) for place in (onward, backward) for offset in last_hops]
    for peer in peers:
        pl.semaphore_signal(barrier, inc=1, device_id=peer, device_id_type=MESH)

    lane = lax.broadcasted_iota(jnp.int32, (rows, rows), 1)
    row = lax.broadcasted_iota(jnp.int32, (rows, rows), 0)
    before = (row < lane).astype(jnp.bfloat16)
    low_row = lax.broadcasted_iota(jnp.int32, (8, part), 0)
    gain = gains_ref[...].astype(jnp.float32)

    def pack_upper(value):
        quarters = [value[:, i * part : (i + 1) * part] for i in range(4)]
        return [jnp.concatenate(quarters[0:2], axis=0), jnp.concatenate(quarters[2:4], axis=0)]

    def pack_lower(value):
        quarters = [value[:, i * part : (i + 1) * part] for i in range(4)]
        halves = [
            jnp.where(low_row < 4, quarters[i], pltpu.roll(quarters[i + 1], 4, 0)) for i in (0, 2)
        ]
        return jnp.concatenate(halves, axis=0)

    def pack(value):
        return pack_upper(value[0:8]) + [pack_lower(value[8:16])]

    def upper_of(pieces):
        return jnp.concatenate([half for p in pieces for half in (p[0:8], p[8:16])], axis=1)

    def lower_of(piece):
        low, high = piece[0:8], piece[8:16]
        return jnp.concatenate([low, pltpu.roll(low, 4, 0), high, pltpu.roll(high, 4, 0)], axis=1)

    def placing(first, second, validity):
        hit = ((first == section) | (second == section)).astype(jnp.float32) * validity
        hit = jnp.broadcast_to(hit, (rows, rows))
        slot = jnp.dot(hit.astype(jnp.bfloat16), before, preferred_element_type=jnp.float32)
        return jnp.where((slot == row.astype(jnp.float32)) & (hit > 0.5), 1.0, 0.0)

    def normalize(x):
        mean_square = jnp.sum(x * x, axis=-1, keepdims=True) * (1.0 / width)
        return x * lax.rsqrt(mean_square + EPSILON) * gain

    def gates(normed, picked, first, second):
        logits = lax.dot_general(
            normed, router_all[...], (((1,), (1,)), ((), ())), preferred_element_type=jnp.float32
        )
        ids = lax.broadcasted_iota(jnp.int32, logits.shape, 1).astype(jnp.float32)
        chosen = [jnp.sum(picked * q.astype(jnp.float32), axis=1, keepdims=True) for q in (first, second)]
        a, b = (jnp.sum(jnp.where(ids == q, logits, 0.0), axis=-1, keepdims=True) for q in chosen)
        first_gate = 1.0 / (1.0 + jnp.exp(b - a))
        second_gate = 1.0 / (1.0 + jnp.exp(a - b))
        window = section.astype(jnp.float32)
        return jnp.where(chosen[0] == window, first_gate, jnp.where(chosen[1] == window, second_gate, 0.0))

    def gather_copy(tick, node, child, sign, piece):
        cols = columns[piece]
        way = 0 if sign > 0 else 1
        return remote(
            gathered.at[tick, PLACE[(node, sign)], :, cols],
            gathered.at[tick, PLACE[(child, sign)], :, cols],
            gather_send.at[tick, way, child, piece],
            gather_recv.at[tick, way, child, piece],
            along(sign * (child - node)),
        )

    def reduce_copy(tick, child, sign, piece):
        cols = columns[piece]
        way = 0 if sign > 0 else 1
        steps = sign * (child - PARENT[child])
        return remote(
            outgoing.at[tick, way, child, :, cols],
            incoming.at[tick, way, child, :, cols],
            reduce_send.at[tick, way, child, piece],
            reduce_recv.at[tick, way, child, piece],
            onward(steps) if tick == 0 and PARENT[child] == 0 else along(steps),
        )

    def both(node, pieces=range(PIECES)):
        return [(piece, sign) for piece in pieces for sign in (1, -1) if travels(node, sign, piece)]

    def arrive(tick, node, pass_on, pieces=range(PIECES)):
        for piece, sign in both(node, pieces):
            gather_copy(tick, PARENT[node], node, sign, piece).wait_recv()
            if pass_on:
                forward(tick, node, piece, sign)

    def forward(tick, node, piece, sign):
        for child in CHILDREN[node]:
            if (child in CHILDREN or node in EAGER) and travels(child, sign, piece):
                gather_copy(tick, node, child, sign, piece).start()

    def forward_leaves(tick, node):
        for child in CHILDREN[node]:
            if child not in CHILDREN and node not in EAGER:
                for piece, sign in both(child):
                    gather_copy(tick, node, child, sign, piece).start()

    def expert(tick, places, parts):
        chunks = [(place, upper) for place in places for upper in parts]
        values = []
        for place, upper in chunks:
            if upper:
                block = gathered[tick, place, :, 0 : 2 * part].astype(jnp.float32)
                values.append(upper_of([block[:, 0:part], block[:, part:]]))
            else:
                values.append(lower_of(gathered[tick, place, :, 2 * part :].astype(jnp.float32)))
        if len(values) % 2:
            values.append(values[-1])
        count = 8 * len(values)
        for i in range(0, len(values), 2):
            unpacked[8 * i : 8 * i + 16, :] = jnp.concatenate(values[i : i + 2], axis=0).astype(jnp.bfloat16)
        tokens = unpacked[0:count, :]
        for begin in range(0, 2 * own_hidden, 256):
            end = min(begin + 256, 2 * own_hidden)
            inner = lax.dot_general(
                tokens, up_all[begin:end, :], (((1,), (1,)), ((), ())), preferred_element_type=jnp.float32
            )
            hidden[0:count, begin:end] = jax.nn.gelu(inner).astype(jnp.bfloat16)
        active = hidden[0:count, :]
        for begin in range(0, width, 512):
            raw[0:count, begin : begin + 512] = jnp.dot(
                active, down_all[:, begin : begin + 512], preferred_element_type=jnp.float32
            )
        for i, (place, upper) in enumerate(chunks):
            rows_out = raw[8 * i : 8 * i + 8, :]
            if upper:
                for k, piece in enumerate(pack_upper(rows_out)):
                    packed_sums[place, :, k * part : (k + 1) * part] = piece
            else:
                packed_sums[place, :, 2 * part :] = pack_lower(rows_out)

    def send_sum(tick, node, pieces=range(PIECES)):
        for piece, sign in both(node, pieces):
            way = 0 if sign > 0 else 1
            cols = columns[piece]
            total = packed_sums[PLACE[(node, -sign)], :, cols]
            for child in CHILDREN.get(node, ()):
                if travels(child, sign, piece):
                    reduce_copy(tick, child, sign, piece).wait_recv()
                    total = total + incoming[tick, way, child, :, cols].astype(jnp.float32)
            outgoing[tick, way, node, :, cols] = total.astype(jnp.bfloat16)
            reduce_copy(tick, node, sign, piece).start()

    def spread_and_sum(tick, normed, meanwhile, weights_ready=None, first_done=None):
        for i, piece in enumerate(pack(normed)):
            gathered[tick, 0, :, i * part : (i + 1) * part] = piece.astype(jnp.bfloat16)
        for piece, sign in both(0):
            forward(tick, 0, piece, sign)
        forward_leaves(tick, 0)
        meanwhile()
        def work(first, last, leaves):
            expert(tick, range(first, last), (True, False))
            if first == 0 and first_done:
                first_done()
            for node in leaves:
                send_sum(tick, node)

        late = []
        for (inner, leaves), (first, last) in zip(STAGES, GROUPS):
            for node in inner:
                arrive(tick, node, True)
                forward_leaves(tick, node)
            if late:
                weights_ready()
                work(*late.pop())
            if inner:
                for node in leaves:
                    arrive(tick, node, False)
                if first == 0 and weights_ready:
                    late.append((first, last, leaves))
                else:
                    work(first, last, leaves)
            else:
                for pieces, upper in (((0, 1), True), ((2,), False)):
                    for node in leaves:
                        arrive(tick, node, False, pieces)
                    expert(tick, range(first, last), (upper,))
                    for node in leaves:
                        send_sum(tick, node, pieces)
        for inner, _ in reversed(STAGES):
            for node in inner:
                send_sum(tick, node)

    def summed(tick, own):
        pieces = []
        for piece in range(PIECES):
            total = own[:, piece * part : (piece + 1) * part].astype(jnp.float32)
            for child in CHILDREN[0]:
                for sign in (1, -1):
                    reduce_copy(tick, child, sign, piece).wait_recv()
                    way = 0 if sign > 0 else 1
                    total = total + incoming[tick, way, child, :, columns[piece]].astype(jnp.float32)
            pieces.append(total)
        lower = lower_of(pieces[2])
        keep = lax.broadcasted_iota(jnp.int32, lower.shape, 0) < CAPACITY - 8
        whole = jnp.concatenate([upper_of(pieces[0:2]), jnp.where(keep, lower, 0.0)], axis=0)
        return whole.astype(jnp.bfloat16).astype(jnp.float32)

    own_length = lengths_ref[0, chip]
    position = core * rows + lane[0:1]
    validity = (position < own_length).astype(jnp.float32)
    first, second = routes_ref[0, 0, 0:1], routes_ref[0, 0, 1:2]
    picked = placing(first, second, validity)
    info[...] = jnp.where(row < 16, picked, validity).astype(jnp.bfloat16)
    picked = picked[0:16]
    loads[0].wait()
    x = jnp.dot(picked.astype(jnp.bfloat16), held[...], preferred_element_type=jnp.float32)
    normed = normalize(x).astype(jnp.bfloat16)
    pl.semaphore_wait(barrier, len(peers))

    swaps = [
        remote(up_ref.at[0], up_all.at[theirs], swap_send.at[0], swap_recv.at[0], sibling),
        remote(down_ref.at[0], down_all.at[theirs], swap_send.at[1], swap_recv.at[1], sibling),
    ]
    shifts = [
        remote(info, info_prev, shift_send.at[0], shift_recv.at[0], following),
        remote(stream_ref.at[0], held_prev, shift_send.at[1], shift_recv.at[1], following),
        remote(gate_out, gate_prev, shift_send.at[2], shift_recv.at[2], following),
        remote(own_sum, own_prev, shift_send.at[3], shift_recv.at[3], following),
    ]
    def first_meanwhile():
        for copy in swaps + shifts[:1]:
            copy.start()
        loads[1].wait()
        gate_out[...] = jnp.broadcast_to(gates(normed, picked, first, second), gate_out.shape)
        shifts[2].start()

    def first_done():
        shifts[1].start()
        own_sum[...] = packed_sums[0].astype(jnp.bfloat16)
        shifts[3].start()

    def weights_ready():
        for load in loads[2:]:
            load.wait()
        for copy in swaps:
            copy.wait_recv()

    spread_and_sum(0, normed.astype(jnp.float32), first_meanwhile, weights_ready, first_done)

    shifts[0].wait_recv()
    prior = info_prev[...].astype(jnp.float32)
    live = prior[64:65] * (section != 0).astype(jnp.float32)
    prior_picked = jnp.where(row < 16, prior, 0.0)
    prior_spread = jnp.transpose(prior_picked)
    renewed_row = jnp.sum(prior_picked, axis=0, keepdims=True)
    renewed = jnp.sum(prior_spread, axis=1, keepdims=True)
    first2, second2 = routes_ref[1, 0, 0:1], routes_ref[1, 0, 1:2]
    picked2 = placing(first2, second2, live)
    spread2 = jnp.transpose(picked2)
    hit2 = jnp.sum(spread2, axis=1, keepdims=True)
    picked2 = picked2[0:16]
    old_rows = (picked2 * (1.0 - renewed_row)).astype(jnp.bfloat16)
    new_rows = jnp.dot(
        picked2.astype(jnp.bfloat16), prior_spread.astype(jnp.bfloat16), preferred_element_type=jnp.float32
    )
    new_rows = new_rows[:, 0:16].astype(jnp.bfloat16)
    shifts[1].wait_recv()
    kept = jnp.dot(old_rows, held_prev[...], preferred_element_type=jnp.float32)

    prior_x = jnp.dot(prior_picked[0:16].astype(jnp.bfloat16), held_prev[...], preferred_element_type=jnp.float32)
    shifts[2].wait_recv()
    prior_gate = gate_prev[:, 0:1]
    shifts[3].wait_recv()
    update = (prior_x + prior_gate * summed(0, own_prev)).astype(jnp.bfloat16)
    x2 = kept + jnp.dot(new_rows, update, preferred_element_type=jnp.float32)
    normed2 = normalize(x2).astype(jnp.bfloat16)

    gate = []

    def second_meanwhile():
        gate.append(gates(normed2, picked2, first2, second2))
        placed = jnp.dot(
            prior_spread[:, 0:16].astype(jnp.bfloat16), update, preferred_element_type=jnp.float32
        ).astype(jnp.bfloat16)
        merged[...] = jnp.where(renewed > 0.5, placed, held_prev[...])

    spread_and_sum(1, normed2.astype(jnp.float32), second_meanwhile)
    final = (x2 + gate[0] * summed(1, packed_sums.at[0])).astype(jnp.bfloat16)
    spread_final = spread2[:, 0:16].astype(jnp.bfloat16)
    struck = hit2 > 0.5
    stores = []
    for i in range(4):
        cols = pl.ds(i * part, part)
        placed = jnp.dot(spread_final, final[:, i * part : (i + 1) * part], preferred_element_type=jnp.float32)
        staged[:, cols] = jnp.where(struck, placed.astype(jnp.bfloat16), merged[:, cols])
        store = pltpu.make_async_copy(staged.at[:, cols], out_ref.at[0, :, cols], out_sem.at[i])
        store.start()
        stores.append(store)
    for tick in (0, 1):
        for child in PARENT:
            for piece, sign in both(child):
                gather_copy(tick, PARENT[child], child, sign, piece).wait_send()
                reduce_copy(tick, child, sign, piece).wait_send()
    for copy in swaps + shifts:
        copy.wait_send()
    for store in stores:
        store.wait()


def shards(stream, lengths, routes, norm_gains, router_weights, up_weights, down_weights):
    rows, width = stream.shape[1:]
    own_hidden = up_weights.shape[2]
    experts = router_weights.shape[2]
    main = width // 4 * 3
    sizes = (lax.axis_size("section"), lax.axis_size("expert"), rows, width, own_hidden)
    bf16, f32 = jnp.bfloat16, jnp.float32
    anywhere = pl.BlockSpec(memory_space=pl.ANY)
    vmem = pl.BlockSpec(memory_space=pltpu.VMEM)
    dma = pltpu.SemaphoreType.DMA
    return pl.pallas_call(
        functools.partial(body, sizes),
        out_shape=jax.ShapeDtypeStruct(stream.shape, bf16),
        in_specs=[anywhere, pl.BlockSpec(memory_space=pltpu.SMEM), vmem, vmem, anywhere, anywhere, anywhere],
        out_specs=anywhere,
        scratch_shapes=[
            pltpu.VMEM((rows, width), bf16),
            pltpu.VMEM((rows, width), bf16),
            pltpu.VMEM((rows, width), bf16),
            pltpu.VMEM((rows, rows), bf16),
            pltpu.VMEM((rows, rows), bf16),
            pltpu.VMEM((2 * own_hidden, width), bf16),
            pltpu.VMEM((2 * own_hidden, width), bf16),
            pltpu.VMEM((experts, width), bf16),
            pltpu.VMEM((2, 16, 16, main), bf16),
            pltpu.VMEM((128, width), bf16),
            pltpu.VMEM((128, 2 * own_hidden), bf16),
            pltpu.VMEM((128, width), f32),
            pltpu.VMEM((16, 16, main), f32),
            pltpu.VMEM((2, 2, 9, 16, main), bf16),
            pltpu.VMEM((2, 2, 9, 16, main), bf16),
            pltpu.VMEM((16, main), bf16),
            pltpu.VMEM((16, main), bf16),
            pltpu.VMEM((16, 128), f32),
            pltpu.VMEM((16, 128), f32),
            pltpu.VMEM((rows, width), bf16),
            dma((4,)),
            dma((2,)),
            dma((2,)),
            dma((4,)),
            dma((4,)),
            dma((2, 2, 9, PIECES)),
            dma((2, 2, 9, PIECES)),
            dma((2, 2, 9, PIECES)),
            dma((2, 2, 9, PIECES)),
            dma((4,)),
        ],
        compiler_params=pltpu.CompilerParams(
            collective_id=0, has_side_effects=True, vmem_limit_bytes=VMEM_LIMIT
        ),
    )(
        stream,
        lengths,
        jnp.swapaxes(routes, 2, 3),
        norm_gains,
        jnp.swapaxes(router_weights, 1, 2),
        jnp.swapaxes(up_weights, 1, 2),
        down_weights,
    )


def solution(mesh):
    in_specs = (
        P("section", "expert", None),
        P("section", None),
        P(None, "section", "expert", None),
        P("section", None),
        P("section", None, None),
        P("section", None, "expert"),
        P("section", "expert", None),
    )
    out_specs = P("section", "expert", None)
    return jax.shard_map(shards, mesh=mesh, in_specs=in_specs, out_specs=out_specs, check_vma=False)
```

```python
import functools

import jax
import jax.numpy as jnp
from jax import lax
from jax.experimental import pallas as pl
from jax.experimental.pallas import tpu as pltpu
from jax.sharding import PartitionSpec as P

MESH = pl.DeviceIdType.MESH
EPSILON = 1e-06
CAPACITY = 12
VMEM_LIMIT = 60 * 1024 * 1024

CHILDREN = {0: (3, 1), 3: (6, 4, 2), 6: (8, 7, 5)}
STAGES = (((3,), (1,)), ((6,), (4, 2)), ((), (8, 7, 5)))
PARENT = {child: node for node, kids in CHILDREN.items() for child in kids}
FAR = 8
EAGER = (6,)


def slot_order():
    order, groups = [(0, 1)], []
    for inner, leaves in STAGES:
        first = len(order) if groups else 0
        for node in inner + leaves:
            order += [(node, 1)] if node == FAR else [(node, 1), (node, -1)]
        groups.append((first, len(order)))
    places = {pair: place for place, pair in enumerate(order)}
    places[(FAR, -1)] = places[(FAR, 1)]
    places[(0, -1)] = 0
    return places, groups


PLACE, GROUPS = slot_order()
PIECES = 3


def travels(node, sign, piece):
    return node != FAR or (piece < 2) == (sign > 0)


OFFSETS = sorted({sign * (child - node) for child, node in PARENT.items() for sign in (1, -1)})


def body(
    sizes,
    stream_ref, lengths_ref, routes_ref, gains_ref, router_ref, up_ref, down_ref,
    out_ref,
    held, held_prev, merged, info, info_prev, up_all, down_all, router_all,
    gathered, unpacked, hidden, raw, packed_sums, outgoing, incoming, own_sum, own_prev, gate_out, gate_prev, staged,
    local_sem, swap_send, swap_recv, shift_send, shift_recv,
    gather_send, gather_recv, reduce_send, reduce_recv, out_sem,
):
    sections, ranks, rows, width, own_hidden = sizes
    main = width // 4 * 3
    part = main // 3
    mine, theirs = pl.ds(0, own_hidden), pl.ds(own_hidden, own_hidden)
    section = lax.axis_index("section")
    rank = lax.axis_index("expert")
    chip, core = rank // 2, lax.rem(rank, 2)
    sibling = (section, rank + 1 - 2 * core)
    forth = 2 - 4 * core
    following = (lax.rem(section + 1, sections), rank)
    previous = (lax.rem(section + sections - 1, sections), rank)

    def along(steps):
        return (section, lax.rem(rank + forth * steps + ranks, ranks))

    def onward(steps):
        return (following[0], lax.rem(rank + forth * steps + ranks, ranks))

    def backward(steps):
        return (previous[0], lax.rem(rank + forth * steps + ranks, ranks))

    columns = [pl.ds(i * part, part) for i in range(PIECES)]

    def remote(src, dst, send, recv, device):
        return pltpu.make_async_remote_copy(
            src_ref=src, dst_ref=dst, send_sem=send, recv_sem=recv, device_id=device, device_id_type=MESH
        )

    loads = [
        pltpu.make_async_copy(stream_ref.at[0], held, local_sem.at[0]),
        pltpu.make_async_copy(router_ref.at[0], router_all, local_sem.at[1]),
        pltpu.make_async_copy(up_ref.at[0], up_all.at[mine], local_sem.at[2]),
        pltpu.make_async_copy(down_ref.at[0], down_all.at[mine], local_sem.at[3]),
    ]
    for load in loads:
        load.start()

    barrier = pltpu.get_barrier_semaphore()
    last_hops = sorted({sign * child for child in CHILDREN[0] for sign in (1, -1)}) + [0]
    peers = [along(offset) for offset in OFFSETS] + [sibling]
    peers += [place(offset) for place in (onward, backward) for offset in last_hops]
    for peer in peers:
        pl.semaphore_signal(barrier, inc=1, device_id=peer, device_id_type=MESH)

    lane = lax.broadcasted_iota(jnp.int32, (rows, rows), 1)
    row = lax.broadcasted_iota(jnp.int32, (rows, rows), 0)
    before = (row < lane).astype(jnp.bfloat16)
    low_row = lax.broadcasted_iota(jnp.int32, (8, part), 0)
    gain = gains_ref[...].astype(jnp.float32)

    def pack_upper(value):
        quarters = [value[:, i * part : (i + 1) * part] for i in range(4)]
        return [jnp.concatenate(quarters[0:2], axis=0), jnp.concatenate(quarters[2:4], axis=0)]

    def pack_lower(value):
        quarters = [value[:, i * part : (i + 1) * part] for i in range(4)]
        halves = [
            jnp.where(low_row < 4, quarters[i], pltpu.roll(quarters[i + 1], 4, 0)) for i in (0, 2)
        ]
        return jnp.concatenate(halves, axis=0)

    def pack(value):
        return pack_upper(value[0:8]) + [pack_lower(value[8:16])]

    def upper_of(pieces):
        return jnp.concatenate([half for p in pieces for half in (p[0:8], p[8:16])], axis=1)

    def lower_of(piece):
        low, high = piece[0:8], piece[8:16]
        return jnp.concatenate([low, pltpu.roll(low, 4, 0), high, pltpu.roll(high, 4, 0)], axis=1)

    def placing(first, second, validity):
        hit = ((first == section) | (second == section)).astype(jnp.float32) * validity
        hit = jnp.broadcast_to(hit, (rows, rows))
        slot = jnp.dot(hit.astype(jnp.bfloat16), before, preferred_element_type=jnp.float32)
        return jnp.where((slot == row.astype(jnp.float32)) & (hit > 0.5), 1.0, 0.0)

    def normalize(x):
        mean_square = jnp.sum(x * x, axis=-1, keepdims=True) * (1.0 / width)
        return x * lax.rsqrt(mean_square + EPSILON) * gain

    def gates(normed, picked, first, second):
        logits = lax.dot_general(
            normed, router_all[...], (((1,), (1,)), ((), ())), preferred_element_type=jnp.float32
        )
        ids = lax.broadcasted_iota(jnp.int32, logits.shape, 1).astype(jnp.float32)
        chosen = [jnp.sum(picked * q.astype(jnp.float32), axis=1, keepdims=True) for q in (first, second)]
        a, b = (jnp.sum(jnp.where(ids == q, logits, 0.0), axis=-1, keepdims=True) for q in chosen)
        first_gate = 1.0 / (1.0 + jnp.exp(b - a))
        second_gate = 1.0 / (1.0 + jnp.exp(a - b))
        window = section.astype(jnp.float32)
        return jnp.where(chosen[0] == window, first_gate, jnp.where(chosen[1] == window, second_gate, 0.0))

    def gather_copy(tick, node, child, sign, piece):
        cols = columns[piece]
        way = 0 if sign > 0 else 1
        return remote(
            gathered.at[tick, PLACE[(node, sign)], :, cols],
            gathered.at[tick, PLACE[(child, sign)], :, cols],
            gather_send.at[tick, way, child, piece],
            gather_recv.at[tick, way, child, piece],
            along(sign * (child - node)),
        )

    def reduce_copy(tick, child, sign, piece):
        cols = columns[piece]
        way = 0 if sign > 0 else 1
        steps = sign * (child - PARENT[child])
        return remote(
            outgoing.at[tick, way, child, :, cols],
            incoming.at[tick, way, child, :, cols],
            reduce_send.at[tick, way, child, piece],
            reduce_recv.at[tick, way, child, piece],
            onward(steps) if tick == 0 and PARENT[child] == 0 else along(steps),
        )

    def both(node, pieces=range(PIECES)):
        return [(piece, sign) for piece in pieces for sign in (1, -1) if travels(node, sign, piece)]

    def arrive(tick, node, pass_on, pieces=range(PIECES)):
        for piece, sign in both(node, pieces):
            gather_copy(tick, PARENT[node], node, sign, piece).wait_recv()
            if pass_on:
                forward(tick, node, piece, sign)

    def forward(tick, node, piece, sign):
        for child in CHILDREN[node]:
            if (child in CHILDREN or node in EAGER) and travels(child, sign, piece):
                gather_copy(tick, node, child, sign, piece).start()

    def forward_leaves(tick, node):
        for child in CHILDREN[node]:
            if child not in CHILDREN and node not in EAGER:
                for piece, sign in both(child):
                    gather_copy(tick, node, child, sign, piece).start()

    def expert(tick, places, parts):
        chunks = [(place, upper) for place in places for upper in parts]
        values = []
        for place, upper in chunks:
            if upper:
                block = gathered[tick, place, :, 0 : 2 * part].astype(jnp.float32)
                values.append(upper_of([block[:, 0:part], block[:, part:]]))
            else:
                values.append(lower_of(gathered[tick, place, :, 2 * part :].astype(jnp.float32)))
        if len(values) % 2:
            values.append(values[-1])
        count = 8 * len(values)
        for i in range(0, len(values), 2):
            unpacked[8 * i : 8 * i + 16, :] = jnp.concatenate(values[i : i + 2], axis=0).astype(jnp.bfloat16)
        tokens = unpacked[0:count, :]
        for begin in range(0, 2 * own_hidden, 256):
            end = min(begin + 256, 2 * own_hidden)
            inner = lax.dot_general(
                tokens, up_all[begin:end, :], (((1,), (1,)), ((), ())), preferred_element_type=jnp.float32
            )
            hidden[0:count, begin:end] = jax.nn.gelu(inner).astype(jnp.bfloat16)
        active = hidden[0:count, :]
        for begin in range(0, width, 512):
            raw[0:count, begin : begin + 512] = jnp.dot(
                active, down_all[:, begin : begin + 512], preferred_element_type=jnp.float32
            )
        for i, (place, upper) in enumerate(chunks):
            rows_out = raw[8 * i : 8 * i + 8, :]
            if upper:
                for k, piece in enumerate(pack_upper(rows_out)):
                    packed_sums[place, :, k * part : (k + 1) * part] = piece
            else:
                packed_sums[place, :, 2 * part :] = pack_lower(rows_out)

    def send_sum(tick, node, pieces=range(PIECES)):
        for piece, sign in both(node, pieces):
            way = 0 if sign > 0 else 1
            cols = columns[piece]
            total = packed_sums[PLACE[(node, -sign)], :, cols]
            for child in CHILDREN.get(node, ()):
                if travels(child, sign, piece):
                    reduce_copy(tick, child, sign, piece).wait_recv()
                    total = total + incoming[tick, way, child, :, cols].astype(jnp.float32)
            outgoing[tick, way, node, :, cols] = total.astype(jnp.bfloat16)
            reduce_copy(tick, node, sign, piece).start()

    def spread_and_sum(tick, normed, meanwhile, weights_ready=None, first_done=None):
        for i, piece in enumerate(pack(normed)):
            gathered[tick, 0, :, i * part : (i + 1) * part] = piece.astype(jnp.bfloat16)
        for piece, sign in both(0):
            forward(tick, 0, piece, sign)
        forward_leaves(tick, 0)
        meanwhile()
        def work(first, last, leaves):
            expert(tick, range(first, last), (True, False))
            if first == 0 and first_done:
                first_done()
            for node in leaves:
                send_sum(tick, node)

        late = []
        for (inner, leaves), (first, last) in zip(STAGES, GROUPS):
            for node in inner:
                arrive(tick, node, True)
                forward_leaves(tick, node)
            if late:
                if weights_ready:
                    weights_ready()
                work(*late.pop())
            if inner:
                for node in leaves:
                    arrive(tick, node, False)
                if first == 0:
                    late.append((first, last, leaves))
                else:
                    work(first, last, leaves)
            else:
                for pieces, upper in (((0, 1), True), ((2,), False)):
                    for node in leaves:
                        arrive(tick, node, False, pieces)
                    expert(tick, range(first, last), (upper,))
                    for node in leaves:
                        send_sum(tick, node, pieces)
        for inner, _ in reversed(STAGES):
            for node in inner:
                send_sum(tick, node)

    def summed(tick, own):
        pieces = []
        for piece in range(PIECES):
            total = own[:, piece * part : (piece + 1) * part].astype(jnp.float32)
            for child in CHILDREN[0]:
                for sign in (1, -1):
                    reduce_copy(tick, child, sign, piece).wait_recv()
                    way = 0 if sign > 0 else 1
                    total = total + incoming[tick, way, child, :, columns[piece]].astype(jnp.float32)
            pieces.append(total)
        lower = lower_of(pieces[2])
        keep = lax.broadcasted_iota(jnp.int32, lower.shape, 0) < CAPACITY - 8
        whole = jnp.concatenate([upper_of(pieces[0:2]), jnp.where(keep, lower, 0.0)], axis=0)
        return whole.astype(jnp.bfloat16).astype(jnp.float32)

    own_length = lengths_ref[0, chip]
    position = core * rows + lane[0:1]
    validity = (position < own_length).astype(jnp.float32)
    first, second = routes_ref[0, 0, 0:1], routes_ref[0, 0, 1:2]
    picked = placing(first, second, validity)
    info[...] = jnp.where(row < 16, picked, validity).astype(jnp.bfloat16)
    picked = picked[0:16]
    loads[0].wait()
    x = jnp.dot(picked.astype(jnp.bfloat16), held[...], preferred_element_type=jnp.float32)
    normed = normalize(x).astype(jnp.bfloat16)
    pl.semaphore_wait(barrier, len(peers))

    swaps = [
        remote(up_ref.at[0], up_all.at[theirs], swap_send.at[0], swap_recv.at[0], sibling),
        remote(down_ref.at[0], down_all.at[theirs], swap_send.at[1], swap_recv.at[1], sibling),
    ]
    shifts = [
        remote(info, info_prev, shift_send.at[0], shift_recv.at[0], following),
        remote(stream_ref.at[0], held_prev, shift_send.at[1], shift_recv.at[1], following),
        remote(gate_out, gate_prev, shift_send.at[2], shift_recv.at[2], following),
        remote(own_sum, own_prev, shift_send.at[3], shift_recv.at[3], following),
    ]
    def first_meanwhile():
        for copy in swaps + shifts[:1]:
            copy.start()
        loads[1].wait()
        gate_out[...] = jnp.broadcast_to(gates(normed, picked, first, second), gate_out.shape)
        shifts[2].start()

    def first_done():
        shifts[1].start()
        own_sum[...] = packed_sums[0].astype(jnp.bfloat16)
        shifts[3].start()

    def weights_ready():
        for load in loads[2:]:
            load.wait()
        for copy in swaps:
            copy.wait_recv()

    spread_and_sum(0, normed.astype(jnp.float32), first_meanwhile, weights_ready, first_done)

    shifts[0].wait_recv()
    prior = info_prev[...].astype(jnp.float32)
    live = prior[64:65] * (section != 0).astype(jnp.float32)
    prior_picked = jnp.where(row < 16, prior, 0.0)
    prior_spread = jnp.transpose(prior_picked)
    renewed_row = jnp.sum(prior_picked, axis=0, keepdims=True)
    renewed = jnp.sum(prior_spread, axis=1, keepdims=True)
    first2, second2 = routes_ref[1, 0, 0:1], routes_ref[1, 0, 1:2]
    picked2 = placing(first2, second2, live)
    spread2 = jnp.transpose(picked2)
    hit2 = jnp.sum(spread2, axis=1, keepdims=True)
    picked2 = picked2[0:16]
    old_rows = (picked2 * (1.0 - renewed_row)).astype(jnp.bfloat16)
    new_rows = jnp.dot(
        picked2.astype(jnp.bfloat16), prior_spread.astype(jnp.bfloat16), preferred_element_type=jnp.float32
    )
    new_rows = new_rows[:, 0:16].astype(jnp.bfloat16)
    shifts[1].wait_recv()
    kept = jnp.dot(old_rows, held_prev[...], preferred_element_type=jnp.float32)

    prior_x = jnp.dot(prior_picked[0:16].astype(jnp.bfloat16), held_prev[...], preferred_element_type=jnp.float32)
    shifts[2].wait_recv()
    prior_gate = gate_prev[:, 0:1]
    shifts[3].wait_recv()
    update = (prior_x + prior_gate * summed(0, own_prev)).astype(jnp.bfloat16)
    x2 = kept + jnp.dot(new_rows, update, preferred_element_type=jnp.float32)
    normed2 = normalize(x2).astype(jnp.bfloat16)

    gate = []

    def second_meanwhile():
        gate.append(gates(normed2, picked2, first2, second2))
        placed = jnp.dot(
            prior_spread[:, 0:16].astype(jnp.bfloat16), update, preferred_element_type=jnp.float32
        ).astype(jnp.bfloat16)
        merged[...] = jnp.where(renewed > 0.5, placed, held_prev[...])

    spread_and_sum(1, normed2.astype(jnp.float32), second_meanwhile)
    final = (x2 + gate[0] * summed(1, packed_sums.at[0])).astype(jnp.bfloat16)
    spread_final = spread2[:, 0:16].astype(jnp.bfloat16)
    struck = hit2 > 0.5
    stores = []
    for i in range(4):
        cols = pl.ds(i * part, part)
        placed = jnp.dot(spread_final, final[:, i * part : (i + 1) * part], preferred_element_type=jnp.float32)
        staged[:, cols] = jnp.where(struck, placed.astype(jnp.bfloat16), merged[:, cols])
        store = pltpu.make_async_copy(staged.at[:, cols], out_ref.at[0, :, cols], out_sem.at[i])
        store.start()
        stores.append(store)
    for tick in (0, 1):
        for child in PARENT:
            for piece, sign in both(child):
                gather_copy(tick, PARENT[child], child, sign, piece).wait_send()
                reduce_copy(tick, child, sign, piece).wait_send()
    for copy in swaps + shifts:
        copy.wait_send()
    for store in stores:
        store.wait()


def shards(stream, lengths, routes, norm_gains, router_weights, up_weights, down_weights):
    rows, width = stream.shape[1:]
    own_hidden = up_weights.shape[2]
    experts = router_weights.shape[2]
    main = width // 4 * 3
    sizes = (lax.axis_size("section"), lax.axis_size("expert"), rows, width, own_hidden)
    bf16, f32 = jnp.bfloat16, jnp.float32
    anywhere = pl.BlockSpec(memory_space=pl.ANY)
    vmem = pl.BlockSpec(memory_space=pltpu.VMEM)
    dma = pltpu.SemaphoreType.DMA
    return pl.pallas_call(
        functools.partial(body, sizes),
        out_shape=jax.ShapeDtypeStruct(stream.shape, bf16),
        in_specs=[anywhere, pl.BlockSpec(memory_space=pltpu.SMEM), vmem, vmem, anywhere, anywhere, anywhere],
        out_specs=anywhere,
        scratch_shapes=[
            pltpu.VMEM((rows, width), bf16),
            pltpu.VMEM((rows, width), bf16),
            pltpu.VMEM((rows, width), bf16),
            pltpu.VMEM((rows, rows), bf16),
            pltpu.VMEM((rows, rows), bf16),
            pltpu.VMEM((2 * own_hidden, width), bf16),
            pltpu.VMEM((2 * own_hidden, width), bf16),
            pltpu.VMEM((experts, width), bf16),
            pltpu.VMEM((2, 16, 16, main), bf16),
            pltpu.VMEM((128, width), bf16),
            pltpu.VMEM((128, 2 * own_hidden), bf16),
            pltpu.VMEM((128, width), f32),
            pltpu.VMEM((16, 16, main), f32),
            pltpu.VMEM((2, 2, 9, 16, main), bf16),
            pltpu.VMEM((2, 2, 9, 16, main), bf16),
            pltpu.VMEM((16, main), bf16),
            pltpu.VMEM((16, main), bf16),
            pltpu.VMEM((16, 128), f32),
            pltpu.VMEM((16, 128), f32),
            pltpu.VMEM((rows, width), bf16),
            dma((4,)),
            dma((2,)),
            dma((2,)),
            dma((4,)),
            dma((4,)),
            dma((2, 2, 9, PIECES)),
            dma((2, 2, 9, PIECES)),
            dma((2, 2, 9, PIECES)),
            dma((2, 2, 9, PIECES)),
            dma((4,)),
        ],
        compiler_params=pltpu.CompilerParams(
            collective_id=0, has_side_effects=True, vmem_limit_bytes=VMEM_LIMIT
        ),
    )(
        stream,
        lengths,
        jnp.swapaxes(routes, 2, 3),
        norm_gains,
        jnp.swapaxes(router_weights, 1, 2),
        jnp.swapaxes(up_weights, 1, 2),
        down_weights,
    )


def solution(mesh):
    in_specs = (
        P("section", "expert", None),
        P("section", None),
        P(None, "section", "expert", None),
        P("section", None),
        P("section", None, None),
        P("section", None, "expert"),
        P("section", "expert", None),
    )
    out_specs = P("section", "expert", None)
    return jax.shard_map(shards, mesh=mesh, in_specs=in_specs, out_specs=out_specs, check_vma=False)
```

```python
import functools

import jax
import jax.numpy as jnp
from jax import lax
from jax.experimental import pallas as pl
from jax.experimental.pallas import tpu as pltpu
from jax.sharding import PartitionSpec as P

MESH = pl.DeviceIdType.MESH
EPSILON = 1e-06
CAPACITY = 12
VMEM_LIMIT = 60 * 1024 * 1024

CHILDREN = {0: (3, 1), 3: (6, 4, 2), 6: (8, 7, 5)}
STAGES = (((3,), (1,)), ((6,), (4, 2)), ((), (8, 7, 5)))
PARENT = {child: node for node, kids in CHILDREN.items() for child in kids}
FAR = 8
EAGER = (6,)


def slot_order():
    order, groups = [(0, 1)], []
    for inner, leaves in STAGES:
        first = len(order) if groups else 0
        for node in inner + leaves:
            order += [(node, 1)] if node == FAR else [(node, 1), (node, -1)]
        groups.append((first, len(order)))
    places = {pair: place for place, pair in enumerate(order)}
    places[(FAR, -1)] = places[(FAR, 1)]
    places[(0, -1)] = 0
    return places, groups


PLACE, GROUPS = slot_order()
PIECES = 2


def travels(node, sign, piece):
    return node != FAR or (piece < 1) == (sign > 0)


OFFSETS = sorted({sign * (child - node) for child, node in PARENT.items() for sign in (1, -1)})


def body(
    sizes,
    stream_ref, lengths_ref, routes_ref, gains_ref, router_ref, up_ref, down_ref,
    out_ref,
    held, held_prev, merged, info, info_prev, up_all, down_all, router_all,
    gathered, unpacked, hidden, raw, packed_sums, outgoing, incoming, own_sum, own_prev, gate_out, gate_prev, staged,
    local_sem, swap_send, swap_recv, shift_send, shift_recv,
    gather_send, gather_recv, reduce_send, reduce_recv, out_sem,
):
    sections, ranks, rows, width, own_hidden = sizes
    main = width // 4 * 3
    part = main // 3
    mine, theirs = pl.ds(0, own_hidden), pl.ds(own_hidden, own_hidden)
    section = lax.axis_index("section")
    rank = lax.axis_index("expert")
    chip, core = rank // 2, lax.rem(rank, 2)
    sibling = (section, rank + 1 - 2 * core)
    forth = 2 - 4 * core
    following = (lax.rem(section + 1, sections), rank)
    previous = (lax.rem(section + sections - 1, sections), rank)

    def along(steps):
        return (section, lax.rem(rank + forth * steps + ranks, ranks))

    def onward(steps):
        return (following[0], lax.rem(rank + forth * steps + ranks, ranks))

    def backward(steps):
        return (previous[0], lax.rem(rank + forth * steps + ranks, ranks))

    spans = ((0, 2 * part), (2 * part, main))
    columns = [pl.ds(begin, end - begin) for begin, end in spans]

    def remote(src, dst, send, recv, device):
        return pltpu.make_async_remote_copy(
            src_ref=src, dst_ref=dst, send_sem=send, recv_sem=recv, device_id=device, device_id_type=MESH
        )

    loads = [
        pltpu.make_async_copy(stream_ref.at[0], held, local_sem.at[0]),
        pltpu.make_async_copy(router_ref.at[0], router_all, local_sem.at[1]),
        pltpu.make_async_copy(up_ref.at[0], up_all.at[mine], local_sem.at[2]),
        pltpu.make_async_copy(down_ref.at[0], down_all.at[mine], local_sem.at[3]),
    ]
    for load in loads:
        load.start()

    barrier = pltpu.get_barrier_semaphore()
    last_hops = sorted({sign * child for child in CHILDREN[0] for sign in (1, -1)}) + [0]
    peers = [along(offset) for offset in OFFSETS] + [sibling]
    peers += [place(offset) for place in (onward, backward) for offset in last_hops]
    for peer in peers:
        pl.semaphore_signal(barrier, inc=1, device_id=peer, device_id_type=MESH)

    lane = lax.broadcasted_iota(jnp.int32, (rows, rows), 1)
    row = lax.broadcasted_iota(jnp.int32, (rows, rows), 0)
    before = (row < lane).astype(jnp.bfloat16)
    low_row = lax.broadcasted_iota(jnp.int32, (8, part), 0)
    gain = gains_ref[...].astype(jnp.float32)

    def pack_upper(value):
        quarters = [value[:, i * part : (i + 1) * part] for i in range(4)]
        return [jnp.concatenate(quarters[0:2], axis=0), jnp.concatenate(quarters[2:4], axis=0)]

    def pack_lower(value):
        quarters = [value[:, i * part : (i + 1) * part] for i in range(4)]
        halves = [
            jnp.where(low_row < 4, quarters[i], pltpu.roll(quarters[i + 1], 4, 0)) for i in (0, 2)
        ]
        return jnp.concatenate(halves, axis=0)

    def pack(value):
        return pack_upper(value[0:8]) + [pack_lower(value[8:16])]

    def upper_of(pieces):
        return jnp.concatenate([half for p in pieces for half in (p[0:8], p[8:16])], axis=1)

    def lower_of(piece):
        low, high = piece[0:8], piece[8:16]
        return jnp.concatenate([low, pltpu.roll(low, 4, 0), high, pltpu.roll(high, 4, 0)], axis=1)

    def placing(first, second, validity):
        hit = ((first == section) | (second == section)).astype(jnp.float32) * validity
        hit = jnp.broadcast_to(hit, (rows, rows))
        slot = jnp.dot(hit.astype(jnp.bfloat16), before, preferred_element_type=jnp.float32)
        return jnp.where((slot == row.astype(jnp.float32)) & (hit > 0.5), 1.0, 0.0)

    def normalize(x):
        mean_square = jnp.sum(x * x, axis=-1, keepdims=True) * (1.0 / width)
        return x * lax.rsqrt(mean_square + EPSILON) * gain

    def gates(normed, picked, first, second):
        logits = lax.dot_general(
            normed, router_all[...], (((1,), (1,)), ((), ())), preferred_element_type=jnp.float32
        )
        ids = lax.broadcasted_iota(jnp.int32, logits.shape, 1).astype(jnp.float32)
        chosen = [jnp.sum(picked * q.astype(jnp.float32), axis=1, keepdims=True) for q in (first, second)]
        a, b = (jnp.sum(jnp.where(ids == q, logits, 0.0), axis=-1, keepdims=True) for q in chosen)
        first_gate = 1.0 / (1.0 + jnp.exp(b - a))
        second_gate = 1.0 / (1.0 + jnp.exp(a - b))
        window = section.astype(jnp.float32)
        return jnp.where(chosen[0] == window, first_gate, jnp.where(chosen[1] == window, second_gate, 0.0))

    def gather_copy(tick, node, child, sign, piece):
        cols = columns[piece]
        way = 0 if sign > 0 else 1
        return remote(
            gathered.at[tick, PLACE[(node, sign)], :, cols],
            gathered.at[tick, PLACE[(child, sign)], :, cols],
            gather_send.at[tick, way, child, piece],
            gather_recv.at[tick, way, child, piece],
            along(sign * (child - node)),
        )

    def reduce_copy(tick, child, sign, piece):
        cols = columns[piece]
        way = 0 if sign > 0 else 1
        steps = sign * (child - PARENT[child])
        return remote(
            outgoing.at[tick, way, child, :, cols],
            incoming.at[tick, way, child, :, cols],
            reduce_send.at[tick, way, child, piece],
            reduce_recv.at[tick, way, child, piece],
            onward(steps) if tick == 0 and PARENT[child] == 0 else along(steps),
        )

    def both(node, pieces=range(PIECES)):
        return [(piece, sign) for piece in pieces for sign in (1, -1) if travels(node, sign, piece)]

    def arrive(tick, node, pass_on, pieces=range(PIECES)):
        for piece, sign in both(node, pieces):
            gather_copy(tick, PARENT[node], node, sign, piece).wait_recv()
            if pass_on:
                forward(tick, node, piece, sign)

    def forward(tick, node, piece, sign):
        for child in CHILDREN[node]:
            if (child in CHILDREN or node in EAGER) and travels(child, sign, piece):
                gather_copy(tick, node, child, sign, piece).start()

    def forward_leaves(tick, node):
        for child in CHILDREN[node]:
            if child not in CHILDREN and node not in EAGER:
                for piece, sign in both(child):
                    gather_copy(tick, node, child, sign, piece).start()

    def expert(tick, places, parts):
        chunks = [(place, upper) for place in places for upper in parts]
        values = []
        for place, upper in chunks:
            if upper:
                block = gathered[tick, place, :, 0 : 2 * part].astype(jnp.float32)
                values.append(upper_of([block[:, 0:part], block[:, part:]]))
            else:
                values.append(lower_of(gathered[tick, place, :, 2 * part :].astype(jnp.float32)))
        if len(values) % 2:
            values.append(values[-1])
        count = 8 * len(values)
        for i in range(0, len(values), 2):
            unpacked[8 * i : 8 * i + 16, :] = jnp.concatenate(values[i : i + 2], axis=0).astype(jnp.bfloat16)
        tokens = unpacked[0:count, :]
        for begin in range(0, 2 * own_hidden, 256):
            end = min(begin + 256, 2 * own_hidden)
            inner = lax.dot_general(
                tokens, up_all[begin:end, :], (((1,), (1,)), ((), ())), preferred_element_type=jnp.float32
            )
            hidden[0:count, begin:end] = jax.nn.gelu(inner).astype(jnp.bfloat16)
        active = hidden[0:count, :]
        for begin in range(0, width, 512):
            raw[0:count, begin : begin + 512] = jnp.dot(
                active, down_all[:, begin : begin + 512], preferred_element_type=jnp.float32
            )
        for i, (place, upper) in enumerate(chunks):
            rows_out = raw[8 * i : 8 * i + 8, :]
            if upper:
                for k, piece in enumerate(pack_upper(rows_out)):
                    packed_sums[place, :, k * part : (k + 1) * part] = piece
            else:
                packed_sums[place, :, 2 * part :] = pack_lower(rows_out)

    def send_sum(tick, node, pieces=range(PIECES)):
        for piece, sign in both(node, pieces):
            way = 0 if sign > 0 else 1
            cols = columns[piece]
            total = packed_sums[PLACE[(node, -sign)], :, cols]
            for child in CHILDREN.get(node, ()):
                if travels(child, sign, piece):
                    reduce_copy(tick, child, sign, piece).wait_recv()
                    total = total + incoming[tick, way, child, :, cols].astype(jnp.float32)
            outgoing[tick, way, node, :, cols] = total.astype(jnp.bfloat16)
            reduce_copy(tick, node, sign, piece).start()

    def spread_and_sum(tick, normed, meanwhile, weights_ready=None, first_done=None):
        for i, piece in enumerate(pack(normed)):
            gathered[tick, 0, :, i * part : (i + 1) * part] = piece.astype(jnp.bfloat16)
        for piece, sign in both(0):
            forward(tick, 0, piece, sign)
        forward_leaves(tick, 0)
        meanwhile()
        def work(first, last, leaves):
            expert(tick, range(first, last), (True, False))
            if first == 0 and first_done:
                first_done()
            for node in leaves:
                send_sum(tick, node)

        late = []
        for (inner, leaves), (first, last) in zip(STAGES, GROUPS):
            for node in inner:
                arrive(tick, node, True)
                forward_leaves(tick, node)
            if late:
                if weights_ready:
                    weights_ready()
                work(*late.pop())
            if inner:
                for node in leaves:
                    arrive(tick, node, False)
                if first == 0:
                    late.append((first, last, leaves))
                else:
                    work(first, last, leaves)
            else:
                for pieces, upper in (((0,), True), ((1,), False)):
                    for node in leaves:
                        arrive(tick, node, False, pieces)
                    expert(tick, range(first, last), (upper,))
                    for node in leaves:
                        send_sum(tick, node, pieces)
        for inner, _ in reversed(STAGES):
            for node in inner:
                send_sum(tick, node)

    def summed(tick, own):
        pieces = []
        for piece in range(PIECES):
            total = own[:, spans[piece][0] : spans[piece][1]].astype(jnp.float32)
            for child in CHILDREN[0]:
                for sign in (1, -1):
                    reduce_copy(tick, child, sign, piece).wait_recv()
                    way = 0 if sign > 0 else 1
                    total = total + incoming[tick, way, child, :, columns[piece]].astype(jnp.float32)
            pieces.append(total)
        lower = lower_of(pieces[1])
        keep = lax.broadcasted_iota(jnp.int32, lower.shape, 0) < CAPACITY - 8
        whole = jnp.concatenate([upper_of([pieces[0][:, 0:part], pieces[0][:, part:]]), jnp.where(keep, lower, 0.0)], axis=0)
        return whole.astype(jnp.bfloat16).astype(jnp.float32)

    own_length = lengths_ref[0, chip]
    position = core * rows + lane[0:1]
    validity = (position < own_length).astype(jnp.float32)
    first, second = routes_ref[0, 0, 0:1], routes_ref[0, 0, 1:2]
    picked = placing(first, second, validity)
    info[...] = jnp.where(row < 16, picked, validity).astype(jnp.bfloat16)
    picked = picked[0:16]
    loads[0].wait()
    x = jnp.dot(picked.astype(jnp.bfloat16), held[...], preferred_element_type=jnp.float32)
    normed = normalize(x).astype(jnp.bfloat16)
    pl.semaphore_wait(barrier, len(peers))

    swaps = [
        remote(up_ref.at[0], up_all.at[theirs], swap_send.at[0], swap_recv.at[0], sibling),
        remote(down_ref.at[0], down_all.at[theirs], swap_send.at[1], swap_recv.at[1], sibling),
    ]
    shifts = [
        remote(info, info_prev, shift_send.at[0], shift_recv.at[0], following),
        remote(stream_ref.at[0], held_prev, shift_send.at[1], shift_recv.at[1], following),
        remote(gate_out, gate_prev, shift_send.at[2], shift_recv.at[2], following),
        remote(own_sum, own_prev, shift_send.at[3], shift_recv.at[3], following),
    ]
    def first_meanwhile():
        for copy in swaps + shifts[:1]:
            copy.start()
        loads[1].wait()
        gate_out[...] = jnp.broadcast_to(gates(normed, picked, first, second), gate_out.shape)
        shifts[2].start()

    def first_done():
        shifts[1].start()
        own_sum[...] = packed_sums[0].astype(jnp.bfloat16)
        shifts[3].start()

    def weights_ready():
        for load in loads[2:]:
            load.wait()
        for copy in swaps:
            copy.wait_recv()

    spread_and_sum(0, normed.astype(jnp.float32), first_meanwhile, weights_ready, first_done)

    shifts[0].wait_recv()
    prior = info_prev[...].astype(jnp.float32)
    live = prior[64:65] * (section != 0).astype(jnp.float32)
    prior_picked = jnp.where(row < 16, prior, 0.0)
    prior_spread = jnp.transpose(prior_picked)
    renewed_row = jnp.sum(prior_picked, axis=0, keepdims=True)
    renewed = jnp.sum(prior_spread, axis=1, keepdims=True)
    first2, second2 = routes_ref[1, 0, 0:1], routes_ref[1, 0, 1:2]
    picked2 = placing(first2, second2, live)
    spread2 = jnp.transpose(picked2)
    hit2 = jnp.sum(spread2, axis=1, keepdims=True)
    picked2 = picked2[0:16]
    old_rows = (picked2 * (1.0 - renewed_row)).astype(jnp.bfloat16)
    new_rows = jnp.dot(
        picked2.astype(jnp.bfloat16), prior_spread.astype(jnp.bfloat16), preferred_element_type=jnp.float32
    )
    new_rows = new_rows[:, 0:16].astype(jnp.bfloat16)
    shifts[1].wait_recv()
    kept = jnp.dot(old_rows, held_prev[...], preferred_element_type=jnp.float32)

    prior_x = jnp.dot(prior_picked[0:16].astype(jnp.bfloat16), held_prev[...], preferred_element_type=jnp.float32)
    shifts[2].wait_recv()
    prior_gate = gate_prev[:, 0:1]
    shifts[3].wait_recv()
    update = (prior_x + prior_gate * summed(0, own_prev)).astype(jnp.bfloat16)
    x2 = kept + jnp.dot(new_rows, update, preferred_element_type=jnp.float32)
    normed2 = normalize(x2).astype(jnp.bfloat16)

    gate = []

    def second_meanwhile():
        gate.append(gates(normed2, picked2, first2, second2))
        placed = jnp.dot(
            prior_spread[:, 0:16].astype(jnp.bfloat16), update, preferred_element_type=jnp.float32
        ).astype(jnp.bfloat16)
        merged[...] = jnp.where(renewed > 0.5, placed, held_prev[...])

    spread_and_sum(1, normed2.astype(jnp.float32), second_meanwhile)
    final = (x2 + gate[0] * summed(1, packed_sums.at[0])).astype(jnp.bfloat16)
    spread_final = spread2[:, 0:16].astype(jnp.bfloat16)
    struck = hit2 > 0.5
    stores = []
    for i in range(4):
        cols = pl.ds(i * part, part)
        placed = jnp.dot(spread_final, final[:, i * part : (i + 1) * part], preferred_element_type=jnp.float32)
        staged[:, cols] = jnp.where(struck, placed.astype(jnp.bfloat16), merged[:, cols])
        store = pltpu.make_async_copy(staged.at[:, cols], out_ref.at[0, :, cols], out_sem.at[i])
        store.start()
        stores.append(store)
    for tick in (0, 1):
        for child in PARENT:
            for piece, sign in both(child):
                gather_copy(tick, PARENT[child], child, sign, piece).wait_send()
                reduce_copy(tick, child, sign, piece).wait_send()
    for copy in swaps + shifts:
        copy.wait_send()
    for store in stores:
        store.wait()


def shards(stream, lengths, routes, norm_gains, router_weights, up_weights, down_weights):
    rows, width = stream.shape[1:]
    own_hidden = up_weights.shape[2]
    experts = router_weights.shape[2]
    main = width // 4 * 3
    sizes = (lax.axis_size("section"), lax.axis_size("expert"), rows, width, own_hidden)
    bf16, f32 = jnp.bfloat16, jnp.float32
    anywhere = pl.BlockSpec(memory_space=pl.ANY)
    vmem = pl.BlockSpec(memory_space=pltpu.VMEM)
    dma = pltpu.SemaphoreType.DMA
    return pl.pallas_call(
        functools.partial(body, sizes),
        out_shape=jax.ShapeDtypeStruct(stream.shape, bf16),
        in_specs=[anywhere, pl.BlockSpec(memory_space=pltpu.SMEM), vmem, vmem, anywhere, anywhere, anywhere],
        out_specs=anywhere,
        scratch_shapes=[
            pltpu.VMEM((rows, width), bf16),
            pltpu.VMEM((rows, width), bf16),
            pltpu.VMEM((rows, width), bf16),
            pltpu.VMEM((rows, rows), bf16),
            pltpu.VMEM((rows, rows), bf16),
            pltpu.VMEM((2 * own_hidden, width), bf16),
            pltpu.VMEM((2 * own_hidden, width), bf16),
            pltpu.VMEM((experts, width), bf16),
            pltpu.VMEM((2, 16, 16, main), bf16),
            pltpu.VMEM((128, width), bf16),
            pltpu.VMEM((128, 2 * own_hidden), bf16),
            pltpu.VMEM((128, width), f32),
            pltpu.VMEM((16, 16, main), f32),
            pltpu.VMEM((2, 2, 9, 16, main), bf16),
            pltpu.VMEM((2, 2, 9, 16, main), bf16),
            pltpu.VMEM((16, main), bf16),
            pltpu.VMEM((16, main), bf16),
            pltpu.VMEM((16, 128), f32),
            pltpu.VMEM((16, 128), f32),
            pltpu.VMEM((rows, width), bf16),
            dma((4,)),
            dma((2,)),
            dma((2,)),
            dma((4,)),
            dma((4,)),
            dma((2, 2, 9, PIECES)),
            dma((2, 2, 9, PIECES)),
            dma((2, 2, 9, PIECES)),
            dma((2, 2, 9, PIECES)),
            dma((4,)),
        ],
        compiler_params=pltpu.CompilerParams(
            collective_id=0, has_side_effects=True, vmem_limit_bytes=VMEM_LIMIT
        ),
    )(
        stream,
        lengths,
        jnp.swapaxes(routes, 2, 3),
        norm_gains,
        jnp.swapaxes(router_weights, 1, 2),
        jnp.swapaxes(up_weights, 1, 2),
        down_weights,
    )


def solution(mesh):
    in_specs = (
        P("section", "expert", None),
        P("section", None),
        P(None, "section", "expert", None),
        P("section", None),
        P("section", None, None),
        P("section", None, "expert"),
        P("section", "expert", None),
    )
    out_specs = P("section", "expert", None)
    return jax.shard_map(shards, mesh=mesh, in_specs=in_specs, out_specs=out_specs, check_vma=False)
```
